32 devices in a mesh: rep: 8 (over z, x), tp: 4 (over y, core).
Axes of the slice: x: 2, y: 2, z: 4, core: 2. Of those that a mesh axis runs over, the one named last changes fastest.
Arguments:
- tokens: bfloat16 [4096, 8192], P('rep', 'tp'), may hold values from -6 to 6
- frozen_weight: bfloat16 [8192, 2048], P('tp'), may hold values from -0.0625 to 0.0625
- cotangent: bfloat16 [4096, 2048], P('rep', 'tp'), may hold values from -6 to 6
- adapter_input_maps: bfloat16 [8, 16, 8192], P('rep', None, 'tp'), may hold values from -0.0625 to 0.0625
- adapter_output_maps: bfloat16 [8, 16, 2048], P('rep', None, 'tp'), may hold values from -0.375 to 0.375
- tenant: int32 [32], P('rep'), may hold values from 0 to 7
- adapter_storage_slot: int32 [8], replicated, may hold values from 0 to 7, each once
Outputs:
- projected: float32 [4096, 2048], P('rep', 'tp')
- token_gradient: float32 [4096, 8192], P('rep', 'tp')
- adapter_input_gradient: float32 [8, 16, 8192], P('rep', None, 'tp')
- adapter_output_gradient: float32 [8, 16, 2048], P('rep', None, 'tp')
The draws below stay inside these ranges and needn't reach their ends.
Inputs may be any that keep to these rules, and one draw needn't show every extreme that they name: `adapter_storage_slot`: each slot holds exactly one adapter.
All inputs are finite; a program needn't handle non-finite values.
Results may differ from the reference program's by a relative error of at most 0.00035.
Values may be sent and summed in bfloat16 or wider, within the bound.
No kernel may reach another device: no remote copies, remote signals or barrier semaphores. Data moves between devices by JAX's collectives and lax.ppermute only.
A program may use at most 64 MiB of HBM per device.

```python
import math
import jax
import jax.numpy as jnp
import numpy as np
from jax import lax

MODEL_WIDTH = 8192
ADAPTER_RANK = 16
BLOCK = 128
KEY_VALUE_WIDTH = 2048
ADAPTER_COUNT = 8
TOKENS = 4096
NBLK = 32


def place_ends(entries, stream_key, least, largest):
    place = [jax.random.randint(jax.random.fold_in(stream_key, axis), (), 0, length) for axis, length in enumerate(entries.shape)]
    main_axis = entries.shape.index(max(entries.shape))
    beside = place[:main_axis] + [(place[main_axis] + 1) % entries.shape[main_axis]] + place[main_axis + 1:]
    return entries.at[tuple(place)].set(least).at[tuple(beside)].set(largest)


def block_scale(stream_key, extent, cuts, least, top_value):
    level = 1.0
    for axis_at, shards_of in cuts:
        steps = jax.random.uniform(jax.random.fold_in(jax.random.fold_in(stream_key, 6), axis_at), (shards_of,), jnp.float32, least / len(cuts), top_value / len(cuts))
        level = level * jnp.repeat(jnp.exp(steps), extent[axis_at] // shards_of).reshape((-1,) + (1,) * (len(extent) - 1 - axis_at))
    return level


def cumulative_ranks(number_of, lean):
    weights = [(1 << 20) // math.isqrt(standing ** lean) + 1 for standing in range(1, number_of + 1)]
    width = 1 + sum(weights) // (1 << 30)
    return np.cumsum(np.array([max(1, weight // width) for weight in weights]))


def ranked_ids(rng, extent, count, lean):
    listing = cumulative_ranks(count, lean)
    ticket = jax.random.randint(jax.random.fold_in(rng, 1), extent, 0, int(listing[count - 1]))
    rank = jnp.searchsorted(jnp.asarray(listing, jnp.int32), ticket, side="right")
    return jax.random.permutation(jax.random.fold_in(rng, 2), count)[rank].astype(jnp.int32)


def centred(rng, shape, spread, most, pieces=(), kind=jnp.bfloat16):
    entries = spread * jax.random.normal(rng, shape, jnp.float32)
    if pieces:
        entries = entries * block_scale(rng, shape, pieces, -0.22, 0.18)
    return jnp.clip(entries, -most, most).astype(kind)


def setup_inputs(seed: int = 0) -> dict:
    keys = jax.random.split(jax.random.key(seed), 8)
    return {
        "tokens": centred(keys[0], (TOKENS, MODEL_WIDTH), 1.0, 6.0, ((0, 8), (1, 4))),
        "frozen_weight": centred(keys[1], (MODEL_WIDTH, KEY_VALUE_WIDTH), MODEL_WIDTH ** -0.5, 0.0625, ((0, 4),)),
        "cotangent": centred(keys[2], (TOKENS, KEY_VALUE_WIDTH), 1.0, 6.0, ((0, 8), (1, 4))),
        "adapter_input_maps": centred(keys[3], (ADAPTER_COUNT, ADAPTER_RANK, MODEL_WIDTH), MODEL_WIDTH ** -0.5, 0.0625, ((0, 8), (2, 4))),
        "adapter_output_maps": centred(keys[4], (ADAPTER_COUNT, ADAPTER_RANK, KEY_VALUE_WIDTH), (16 * ADAPTER_RANK) ** -0.5, 0.375, ((0, 8), (2, 4))),
        "tenant": place_ends(ranked_ids(keys[5], (NBLK,), ADAPTER_COUNT, 2), jax.random.fold_in(keys[5], 3), 0, ADAPTER_COUNT - 1).astype(jnp.int32),
        "adapter_storage_slot": jax.random.permutation(keys[6], ADAPTER_COUNT).astype(jnp.int32),
    }


HIGH_ACCURACY = lax.Precision.HIGHEST


def reference(tokens, frozen_weight, cotangent, adapter_input_maps, adapter_output_maps, tenant, adapter_storage_slot):
    adapter_list = adapter_input_maps.shape[0]
    blocks = tenant.shape[0]
    block_storage_slot = adapter_storage_slot[tenant]
    input_map_rows = adapter_input_maps[block_storage_slot].astype(jnp.float32)
    output_map_rows = adapter_output_maps[block_storage_slot].astype(jnp.float32)
    token_rows = tokens.reshape(blocks, BLOCK, MODEL_WIDTH).astype(jnp.float32)
    rank_in = jnp.einsum('bnd,brd->bnr', token_rows, input_map_rows, precision=HIGH_ACCURACY)
    base = jnp.dot(tokens, frozen_weight, preferred_element_type=jnp.float32)
    low_rank = 2.0 * jnp.einsum('bnr,brc->bnc', rank_in, output_map_rows, precision=HIGH_ACCURACY)
    projected = base + low_rank.reshape(-1, KEY_VALUE_WIDTH)
    grad_rows = cotangent.reshape(blocks, BLOCK, KEY_VALUE_WIDTH).astype(jnp.float32)
    rank_back = jnp.einsum('bnc,brc->bnr', grad_rows, output_map_rows, precision=HIGH_ACCURACY)
    through = jnp.dot(cotangent, frozen_weight.T, preferred_element_type=jnp.float32)
    side = 2.0 * jnp.einsum('bnr,brd->bnd', rank_back, input_map_rows, precision=HIGH_ACCURACY)
    token_gradient = through + side.reshape(-1, MODEL_WIDTH)
    input_map_gradient = 2.0 * jnp.einsum('bnr,bnd->brd', rank_back, token_rows, precision=HIGH_ACCURACY)
    output_map_gradient = 2.0 * jnp.einsum('bnr,bnc->brc', rank_in, grad_rows, precision=HIGH_ACCURACY)
    tenant_selector = (block_storage_slot[:, None] == jnp.arange(adapter_list, dtype=jnp.int32)[None, :]).astype(jnp.float32)
    counts = BLOCK * jnp.sum(tenant_selector, axis=0)
    adapter_scale = 1.0 / jnp.maximum(counts, 1.0)
    adapter_input_gradient = jnp.einsum('ol,oht->lht', tenant_selector, input_map_gradient, precision=HIGH_ACCURACY) * adapter_scale[:, None, None]
    adapter_output_gradient = jnp.einsum('pa,pne->ane', tenant_selector, output_map_gradient, precision=HIGH_ACCURACY) * adapter_scale[:, None, None]
    return (projected, token_gradient, adapter_input_gradient, adapter_output_gradient)
```

```python
import functools

import jax
import jax.numpy as jnp
from jax import lax
from jax.experimental import pallas as pl
from jax.experimental.pallas import tpu as pltpu
from jax.sharding import PartitionSpec as P

F32, BF16, I32, I16 = jnp.float32, jnp.bfloat16, jnp.int32, jnp.int16
VM = pltpu.VMEM
STEPS = 128.0
CODE_TOP = 32767.0
LEAST = 1e-33
LANES = 128
COUNT_LANE = 64
NT = (((1,), (1,)), ((), ()))
TN = (((0,), (0,)), ((), ()))


def params(mib, grid_dims=0):
    return pltpu.CompilerParams(
        vmem_limit_bytes=mib << 20,
        dimension_semantics=("arbitrary",) * grid_dims if grid_dims else None,
    )


def cost(flops, moved):
    return pl.CostEstimate(flops=int(flops), bytes_accessed=int(moved), transcendentals=0)


def whole(n):
    return [pl.BlockSpec(memory_space=VM)] * n


def scale_code(top):
    return jnp.ceil(STEPS * (jnp.log2(jnp.maximum(top, LEAST)) - 15.0)) + 1.0


def to_code(value, code):
    level = jnp.round(value * jnp.exp2(code * (-1.0 / STEPS)))
    return jnp.clip(level, -CODE_TOP, CODE_TOP).astype(I32).astype(I16)


def from_code(level, code):
    return level.astype(I32).astype(F32) * jnp.exp2(code.astype(I32).astype(F32) * (1.0 / STEPS))


def split(value):
    high = value.astype(BF16)
    return high, (value - high.astype(F32)).astype(BF16)


def base_send_kernel(order, x_ref, w_ref, out_ref):
    out_ref[0] = jnp.dot(x_ref[...], w_ref[...], preferred_element_type=F32)


def base_keep_kernel(group, blocks, order, x_ref, w_ref, got_ref, own_ref, code_ref):
    k = pl.program_id(0)
    total = jnp.dot(x_ref[...], w_ref[...], preferred_element_type=F32) + got_ref[0]
    rows = total.shape[0]

    @pl.when(k == 0)
    def _():
        own_ref[...] = total

    @pl.when(k > 0)
    def _():
        tail = jnp.zeros((16, total.shape[1]), F32)
        row = lax.broadcasted_iota(I32, tail.shape, 0)
        for g in range(rows // group):
            part = total[g * group : (g + 1) * group]
            code = scale_code(jnp.max(jnp.abs(part), axis=0, keepdims=True))
            code_ref[0, g * group : (g + 1) * group, :] = to_code(part, code)
            tail = jnp.where(row == g, code, tail)
        code_ref[0, rows:, :] = tail.astype(I32).astype(I16)


def base_send(order, x, w, chips, width):
    rows, depth = x.shape
    block = min(256, width)
    per = width // block
    return pl.pallas_call(
        base_send_kernel,
        grid_spec=pltpu.PrefetchScalarGridSpec(
            num_scalar_prefetch=1,
            grid=(chips, per),
            in_specs=[
                pl.BlockSpec((rows, depth), lambda k, j, o: (0, 0)),
                pl.BlockSpec((depth, block), lambda k, j, o: (0, o[k] * per + j)),
            ],
            out_specs=pl.BlockSpec((1, rows, block), lambda k, j, o: (k, 0, j)),
        ),
        out_shape=jax.ShapeDtypeStruct((chips, rows, width), F32),
        compiler_params=params(24, 2),
        cost_estimate=cost(2 * rows * depth * chips * width, 2 * rows * depth + 2 * depth * chips * width),
        name="base_send",
    )(order, x, w)


def base_keep(order, x, w, got, chips, width, group):
    rows, depth = x.shape
    block = min(256, width)
    per = width // block
    return pl.pallas_call(
        functools.partial(base_keep_kernel, group, per),
        grid_spec=pltpu.PrefetchScalarGridSpec(
            num_scalar_prefetch=1,
            grid=(chips, per),
            in_specs=[
                pl.BlockSpec((rows, depth), lambda k, j, o: (0, 0)),
                pl.BlockSpec((depth, block), lambda k, j, o: (0, o[k] * per + j)),
                pl.BlockSpec((1, rows, block), lambda k, j, o: (k, 0, j)),
            ],
            out_specs=[
                pl.BlockSpec((rows, block), lambda k, j, o: (0, jnp.where(k == 0, j, per - 1))),
                pl.BlockSpec(
                    (1, rows + 16, block),
                    lambda k, j, o: (jnp.maximum(k - 1, 0), 0, jnp.where(k == 0, 0, j)),
                ),
            ],
        ),
        out_shape=[
            jax.ShapeDtypeStruct((rows, width), F32),
            jax.ShapeDtypeStruct((chips - 1, rows + 16, width), I16),
        ],
        compiler_params=params(24, 2),
        cost_estimate=cost(2 * rows * depth * chips * width, 2 * rows * depth + 2 * depth * chips * width),
        name="base_keep",
    )(order, x, w, got)


def gather_pieces(pieces, table):
    at = 0
    for piece in pieces:
        table[at : at + piece.shape[0]] = piece[...]
        at += piece.shape[0]


def rank_kernel(blocks, pieces, place, v_ref, *refs):
    maps, out_ref, table = refs[:pieces], refs[pieces], refs[pieces + 1]
    gather_pieces(maps, table)
    length = v_ref.shape[0] // blocks
    for b in range(blocks):
        out_ref[:, b * length : (b + 1) * length] = lax.dot_general(
            table[place[b]], v_ref[b * length : (b + 1) * length], NT, preferred_element_type=F32
        )


def rank_part(place, v, maps, blocks):
    rows, width = v.shape
    count = sum(m.shape[0] for m in maps)
    rank = maps[0].shape[1]
    return pl.pallas_call(
        functools.partial(rank_kernel, blocks, len(maps)),
        in_specs=[pl.BlockSpec(memory_space=pltpu.SMEM)] + whole(1 + len(maps)),
        out_specs=whole(1)[0],
        out_shape=jax.ShapeDtypeStruct((rank, rows), F32),
        scratch_shapes=[VM((count, rank, width), BF16)],
        compiler_params=params(16),
        cost_estimate=cost(2 * rows * width * 128, 2 * rows * width),
        name="rank_part",
    )(place, v, *maps)


def encode_rows(value, count, out_ref, at):
    rank, width = value.shape
    group = min(512, width)
    tail = jnp.zeros((rank, LANES), F32)
    lane = lax.broadcasted_iota(I32, tail.shape, 1)
    for g in range(width // group):
        part = value[:, g * group : (g + 1) * group]
        code = scale_code(jnp.max(jnp.abs(part), axis=1, keepdims=True))
        out_ref[at, :, g * group : (g + 1) * group] = to_code(part, code)
        tail = jnp.where(lane == g, code, tail)
    tail = jnp.where(lane == COUNT_LANE, count, tail)
    out_ref[at, :, width:] = tail.astype(I32).astype(I16)


def decode_rows(ref, at, width):
    group = min(512, width)
    tail = ref[at, :, width:].astype(I32).astype(F32)
    parts = []
    for g in range(width // group):
        level = ref[at, :, g * group : (g + 1) * group].astype(I32).astype(F32)
        parts.append(level * jnp.exp2(tail[:, g : g + 1] * (1.0 / STEPS)))
    return jnp.concatenate(parts, axis=1), tail[:, COUNT_LANE : COUNT_LANE + 1]


def table_kernel(blocks, terms, slots, place, v_ref, *refs):
    ranks, (send_ref, keep_ref, table) = refs[:terms], refs[terms:]
    rank_total = ranks[0][...]
    for term in ranks[1:]:
        rank_total = rank_total + term[...]
    high, low = split(rank_total)
    rank = rank_total.shape[0]
    width = v_ref.shape[1]
    length = v_ref.shape[0] // blocks
    table[...] = jnp.zeros_like(table)
    both = jnp.concatenate([high, low], axis=0)
    for b in range(blocks):
        cut = slice(b * length, (b + 1) * length)
        outer = jnp.dot(both[:, cut], v_ref[cut], preferred_element_type=F32)
        table[place[b]] += outer[:rank] + outer[rank:]
    for m in range(slots):
        count = jnp.int32(0)
        for b in range(blocks):
            count += (place[b] == m).astype(I32)
        count = count.astype(F32)
        if m % 2:
            encode_rows(table[m], count, send_ref, m // 2)
        else:
            keep_ref[m // 2, :, :width] = table[m]
            keep_ref[m // 2, :, width:] = jnp.full((rank, LANES), count, F32)


def table_sums(place, v, ranks, blocks, slots):
    rows, width = v.shape
    rank = ranks[0].shape[0]
    half = slots // 2
    return pl.pallas_call(
        functools.partial(table_kernel, blocks, len(ranks), slots),
        in_specs=[pl.BlockSpec(memory_space=pltpu.SMEM)] + whole(1 + len(ranks)),
        out_specs=whole(2),
        out_shape=[
            jax.ShapeDtypeStruct((half, rank, width + LANES), I16),
            jax.ShapeDtypeStruct((half, rank, width + LANES), F32),
        ],
        scratch_shapes=[VM((slots, rank, width), F32)],
        compiler_params=params(24),
        cost_estimate=cost(4 * rows * width * 32, 2 * rows * width),
        name="table_sums",
    )(place, v, *ranks)


def combine_kernel(keep_ref, got_ref, own_ref, *sends):
    width = keep_ref.shape[2] - LANES
    for j in range(keep_ref.shape[0]):
        value, count = decode_rows(got_ref, j, width)
        value = value + keep_ref[j, :, :width]
        count = count + keep_ref[j, :, width : width + 1]
        if j == 0:
            own_ref[0, :, :width] = value
            own_ref[0, :, width:] = jnp.broadcast_to(count, (count.shape[0], LANES))
        else:
            encode_rows(value, count, sends[j - 1], 0)


def combine(keep, got):
    half, rank, wide = keep.shape
    return pl.pallas_call(
        combine_kernel,
        in_specs=whole(2),
        out_specs=whole(half),
        out_shape=[jax.ShapeDtypeStruct((1, rank, wide), F32)]
        + [jax.ShapeDtypeStruct((1, rank, wide), I16)] * (half - 1),
        compiler_params=params(16),
        cost_estimate=cost(half * rank * wide * 16, half * rank * wide * 8),
        name="combine",
    )(keep, got)


def finish_kernel(block_length, own_ref, *refs):
    gots, out_ref = refs[:-1], refs[-1]
    width = own_ref.shape[2] - LANES
    value, count = own_ref[0, :, :width], own_ref[0, :, width : width + 1]
    for got in gots:
        more, further = decode_rows(got, 0, width)
        value, count = value + more, count + further
    out_ref[0] = value * (2.0 / jnp.maximum(count * float(block_length), 1.0))


def finish(own, gots, block_length):
    _, rank, wide = own.shape
    return pl.pallas_call(
        functools.partial(finish_kernel, block_length),
        in_specs=whole(1 + len(gots)),
        out_specs=whole(1)[0],
        out_shape=jax.ShapeDtypeStruct((1, rank, wide - LANES), F32),
        compiler_params=params(16),
        cost_estimate=cost(rank * wide * 32, rank * wide * 16),
        name="finish",
    )(own, *gots)


def low_rank(both, maps):
    return lax.dot_general(both, jnp.concatenate([maps, maps], axis=0), TN, preferred_element_type=F32)


def through_kernel(blocks, cots, terms, pieces, order, place, *refs):
    cot_refs, refs = refs[:cots], refs[cots:]
    w_ref, refs = refs[0], refs[1:]
    ranks, refs = refs[:terms], refs[terms:]
    maps, (out_ref, table) = refs[:pieces], refs[pieces:]
    gather_pieces(maps, table)
    rank_total = ranks[0][...]
    for term in ranks[1:]:
        rank_total = rank_total + term[...]
    both = jnp.concatenate(split(2.0 * rank_total), axis=0)
    width = cot_refs[0].shape[1]
    length = cot_refs[0].shape[0] // blocks
    total = None
    for i, cot in enumerate(cot_refs):
        columns = pl.ds(pl.multiple_of(order[i] * width, width), width)
        term = lax.dot_general(cot[...], w_ref[:, columns], NT, preferred_element_type=F32)
        total = term if total is None else total + term
    for b in range(blocks):
        cut = slice(b * length, (b + 1) * length)
        out_ref[cut] = total[cut] + low_rank(both[:, cut], table[place[b]])


def through(order, place, cots, w, ranks, maps, blocks):
    rows, width = cots[0].shape
    depth, features = w.shape
    count = sum(m.shape[0] for m in maps)
    rank = maps[0].shape[1]
    block = min(256, depth)
    return pl.pallas_call(
        functools.partial(through_kernel, blocks, len(cots), len(ranks), len(maps)),
        grid_spec=pltpu.PrefetchScalarGridSpec(
            num_scalar_prefetch=2,
            grid=(depth // block,),
            in_specs=[pl.BlockSpec((rows, width), lambda i, *_: (0, 0)) for _ in cots]
            + [pl.BlockSpec((block, features), lambda i, *_: (i, 0))]
            + [pl.BlockSpec((rank, rows), lambda i, *_: (0, 0)) for _ in ranks]
            + [pl.BlockSpec((m.shape[0], rank, block), lambda i, *_: (0, 0, i)) for m in maps],
            out_specs=pl.BlockSpec((rows, block), lambda i, *_: (0, i)),
            scratch_shapes=[VM((count, rank, block), BF16)],
        ),
        out_shape=jax.ShapeDtypeStruct((rows, depth), F32),
        compiler_params=params(24, 1),
        cost_estimate=cost(2 * rows * depth * features, 2 * depth * features + 4 * rows * depth),
        name="through",
    )(order, place, *cots, w, *ranks, *maps)


def project_kernel(blocks, group, codes, terms, pieces, place, own_ref, *refs):
    code_refs, refs = refs[:codes], refs[codes:]
    ranks, refs = refs[:terms], refs[terms:]
    maps, (out_ref, table) = refs[:pieces], refs[pieces:]
    gather_pieces(maps, table)
    rank_total = ranks[0][...]
    for term in ranks[1:]:
        rank_total = rank_total + term[...]
    both = jnp.concatenate(split(2.0 * rank_total), axis=0)
    rows = own_ref.shape[0]
    length = rows // blocks
    for b in range(blocks):
        cut = slice(b * length, (b + 1) * length)
        total = own_ref[cut] + low_rank(both[:, cut], table[place[b]])
        for code in code_refs:
            g = b * length // group
            scale = jnp.exp2(code[0, rows : rows + 16].astype(I32).astype(F32) * (1.0 / STEPS))
            total = total + code[0, cut].astype(I32).astype(F32) * scale[g : g + 1]
        out_ref[cut] = total


def project(place, own, codes, ranks, maps, blocks, group):
    rows, width = own.shape
    count = sum(m.shape[0] for m in maps)
    rank = maps[0].shape[1]
    return pl.pallas_call(
        functools.partial(project_kernel, blocks, group, len(codes), len(ranks), len(maps)),
        in_specs=[pl.BlockSpec(memory_space=pltpu.SMEM)] + whole(1 + len(codes) + len(ranks) + len(maps)),
        out_specs=whole(1)[0],
        out_shape=jax.ShapeDtypeStruct((rows, width), F32),
        scratch_shapes=[VM((count, rank, width), BF16)],
        compiler_params=params(24),
        cost_estimate=cost(2 * rows * width * 64, rows * width * 8),
        name="project",
    )(place, own, *codes, *ranks, *maps)


def swap(value, axis, size, mask):
    return lax.ppermute(value, axis, [(i, i ^ mask) for i in range(size)])


def shards(reps, tps, tokens, weight, cot, maps_in, maps_out, tenant, slot_of):
    chips = tps // 2
    blocks = tenant.shape[0]
    rows = tokens.shape[0]
    length = rows // blocks
    slots = reps
    width = cot.shape[1]
    rep, tp = lax.axis_index("rep"), lax.axis_index("tp")
    core = functools.partial(swap, axis="tp", size=tps, mask=1)

    def over_y(value, k):
        return swap(value, "tp", tps, 2 * k)

    def over_rep(value, mask):
        return swap(value, "rep", reps, mask)

    labels = jnp.arange(slot_of.shape[0], dtype=I32)
    slot = jnp.sum(jnp.where(tenant[:, None] == labels[None, :], slot_of[None, :], 0), axis=1)
    place = jnp.bitwise_xor(slot, rep.astype(I32)).astype(I32)
    chip_at = 2 * jnp.arange(chips, dtype=I32)
    keep_order = jnp.bitwise_xor(chip_at, tp.astype(I32))
    send_order = jnp.bitwise_xor(keep_order, 1)

    cot_y = [over_y(cot, k) for k in range(1, chips)]
    cot_c = core(cot)

    def gather(own):
        pair = jnp.concatenate([own, over_rep(own, 1)], axis=0)
        return [pair] + [over_rep(pair, m) for m in range(2, reps, 2)]

    outs_all = gather(maps_out)
    ins_all = gather(maps_in)

    sent = base_send(send_order, tokens, weight, chips, width)
    got = core(sent)
    own_base, codes = base_keep(keep_order, tokens, weight, got, chips, width, 128)

    def rank_sums(v, maps):
        part = rank_part(place, v, maps, blocks)
        chip_sum = part + core(part)
        return [chip_sum] + [over_y(chip_sum, k) for k in range(1, chips)]

    back = rank_sums(cot, outs_all)
    base_codes = [over_y(codes[k - 1 : k], k) for k in range(1, chips)]
    forward = rank_sums(tokens, ins_all)

    def reduce(v, ranks):
        send, keep = table_sums(place, v, ranks, blocks, slots)
        own, *sends = combine(keep, over_rep(send, 1))
        gots = [over_rep(s, 2 * (j + 1)) for j, s in enumerate(sends)]
        return finish(own, gots, length)

    grad_in = reduce(tokens, back)
    cots, cot_order = [cot, cot_c], [keep_order[0], send_order[0]]
    for k, piece in enumerate(cot_y):
        cots += [piece, core(piece)]
        cot_order += [keep_order[k + 1], send_order[k + 1]]
    token_grad = through(jnp.stack(cot_order), place, cots, weight, back, ins_all, blocks)
    grad_out = reduce(cot, forward)
    projected = project(place, own_base, base_codes, forward, outs_all, blocks, 128)
    return projected, token_grad, grad_in, grad_out


def solution(mesh):
    placed = (
        P("rep", "tp"),
        P("tp", None),
        P("rep", "tp"),
        P("rep", None, "tp"),
        P("rep", None, "tp"),
        P("rep"),
        P(),
    )
    return jax.shard_map(
        functools.partial(shards, mesh.shape["rep"], mesh.shape["tp"]),
        mesh=mesh,
        in_specs=placed,
        out_specs=(P("rep", "tp"), P("rep", "tp"), P("rep", None, "tp"), P("rep", None, "tp")),
        check_vma=False,
    )
```

```python
import functools

import jax
import jax.numpy as jnp
from jax import lax
from jax.experimental import pallas as pl
from jax.experimental.pallas import tpu as pltpu
from jax.sharding import PartitionSpec as P

F32, BF16, I32, I16 = jnp.float32, jnp.bfloat16, jnp.int32, jnp.int16
VM = pltpu.VMEM
STEPS = 128.0
CODE_TOP = 32767.0
LEAST = 1e-33
LANES = 128
COUNT_LANE = 64
NT = (((1,), (1,)), ((), ()))
TN = (((0,), (0,)), ((), ()))


def params(mib, grid_dims=0):
    return pltpu.CompilerParams(
        vmem_limit_bytes=mib << 20,
        dimension_semantics=("arbitrary",) * grid_dims if grid_dims else None,
    )


def cost(flops, moved):
    return pl.CostEstimate(flops=int(flops), bytes_accessed=int(moved), transcendentals=0)


def whole(n):
    return [pl.BlockSpec(memory_space=VM)] * n


def scale_code(top):
    return jnp.ceil(STEPS * (jnp.log2(jnp.maximum(top, LEAST)) - 15.0)) + 1.0


def to_code(value, code):
    level = jnp.round(value * jnp.exp2(code * (-1.0 / STEPS)))
    return jnp.clip(level, -CODE_TOP, CODE_TOP).astype(I32).astype(I16)


def from_code(level, code):
    return level.astype(I32).astype(F32) * jnp.exp2(code.astype(I32).astype(F32) * (1.0 / STEPS))


def split(value):
    high = value.astype(BF16)
    return high, (value - high.astype(F32)).astype(BF16)


def plan_kernel(ids, tenant, slot_of, place, order):
    for b in range(place.shape[0]):
        place[b] = jnp.bitwise_xor(slot_of[tenant[b]], ids[0])
    for i in range(order.shape[0]):
        order[i] = jnp.bitwise_xor(ids[1], i)


def plan(rep, tp, tenant, slot_of, tps):
    smem = pl.BlockSpec(memory_space=pltpu.SMEM)
    ids = jnp.stack([rep, tp]).astype(I32)
    return pl.pallas_call(
        plan_kernel,
        in_specs=[smem] * 3,
        out_specs=[smem] * 2,
        out_shape=[jax.ShapeDtypeStruct(tenant.shape, I32), jax.ShapeDtypeStruct((tps,), I32)],
        compiler_params=params(1),
        cost_estimate=cost(10e9, 0),
        name="plan",
    )(ids, tenant, slot_of)


def base_send_kernel(masks, order, x_ref, w_ref, out_ref):
    width = out_ref.shape[2]
    for i, mask in enumerate(masks):
        columns = pl.ds(pl.multiple_of(order[mask] * width, width), width)
        out_ref[i] = jnp.dot(x_ref[...], w_ref[:, columns], preferred_element_type=F32)


def base_send(order, x, w, masks, width):
    rows, depth = x.shape
    return pl.pallas_call(
        functools.partial(base_send_kernel, masks),
        in_specs=[pl.BlockSpec(memory_space=pltpu.SMEM)] + whole(2),
        out_specs=whole(1)[0],
        out_shape=jax.ShapeDtypeStruct((len(masks), rows, width), F32),
        compiler_params=params(8),
        cost_estimate=cost(0, 0),
        name="base_send",
    )(order, x, w)


def base_own_kernel(order, x_ref, w_ref, got_ref, own_ref):
    width = own_ref.shape[1]
    columns = pl.ds(pl.multiple_of(order[0] * width, width), width)
    own_ref[...] = got_ref[0] + jnp.dot(x_ref[...], w_ref[:, columns], preferred_element_type=F32)


def base_own(order, x, w, got):
    _, rows, width = got.shape
    return pl.pallas_call(
        base_own_kernel,
        in_specs=[pl.BlockSpec(memory_space=pltpu.SMEM)] + whole(3),
        out_specs=whole(1)[0],
        out_shape=jax.ShapeDtypeStruct((rows, width), F32),
        compiler_params=params(8),
        cost_estimate=cost(0, 0),
        name="base_own",
    )(order, x, w, got)


def base_code_kernel(group, masks, order, x_ref, w_ref, got_ref, *code_refs):
    rows, width = got_ref.shape[1:]
    block = min(256, width)
    for i, (mask, code_ref) in enumerate(zip(masks, code_refs)):
        for j in range(width // block):
            cut = slice(j * block, (j + 1) * block)
            columns = pl.ds(pl.multiple_of(order[mask] * width + j * block, block), block)
            total = got_ref[i, :, cut] + jnp.dot(x_ref[...], w_ref[:, columns], preferred_element_type=F32)
            tail = jnp.zeros((16, block), F32)
            row = lax.broadcasted_iota(I32, tail.shape, 0)
            for g in range(rows // group):
                part = total[g * group : (g + 1) * group]
                code = scale_code(jnp.max(jnp.abs(part), axis=0, keepdims=True))
                code_ref[0, g * group : (g + 1) * group, cut] = to_code(part, code)
                tail = jnp.where(row == g, code, tail)
            code_ref[0, rows:, cut] = tail.astype(I32).astype(I16)


def base_code(order, x, w, got, masks, group):
    count, rows, width = got.shape
    return pl.pallas_call(
        functools.partial(base_code_kernel, group, masks),
        in_specs=[pl.BlockSpec(memory_space=pltpu.SMEM)] + whole(3),
        out_specs=whole(count),
        out_shape=[jax.ShapeDtypeStruct((1, rows + 16, width), I16)] * count,
        compiler_params=params(12),
        cost_estimate=cost(0, 0),
        name="base_code",
    )(order, x, w, got)


def gather_masks(count):
    masks, bit = [0], count // 2
    while bit:
        masks, bit = masks + [m ^ bit for m in masks], bit // 2
    return masks


def gather_pieces(pieces, table):
    masks = iter(gather_masks(table.shape[0]))
    for piece in pieces:
        for i in range(piece.shape[0]):
            table[next(masks)] = piece[i]


def rank_kernel(blocks, pieces, place, v_ref, *refs):
    maps, out_ref, table = refs[:pieces], refs[pieces], refs[pieces + 1]
    gather_pieces(maps, table)
    length = v_ref.shape[0] // blocks
    for b in range(blocks):
        out_ref[:, b * length : (b + 1) * length] = lax.dot_general(
            table[place[b]], v_ref[b * length : (b + 1) * length], NT, preferred_element_type=F32
        )


def rank_part(place, v, maps, blocks):
    rows, width = v.shape
    count = sum(m.shape[0] for m in maps)
    rank = maps[0].shape[1]
    return pl.pallas_call(
        functools.partial(rank_kernel, blocks, len(maps)),
        in_specs=[pl.BlockSpec(memory_space=pltpu.SMEM)] + whole(1 + len(maps)),
        out_specs=whole(1)[0],
        out_shape=jax.ShapeDtypeStruct((rank, rows), F32),
        scratch_shapes=[VM((count, rank, width), BF16)],
        compiler_params=params(4),
        cost_estimate=cost(0, 0),
        name="rank_part",
    )(place, v, *maps)


def encode_rows(value, count, out_ref, at, start=0):
    rank, width = value.shape
    group = min(512, width)
    tail = jnp.zeros((rank, LANES), F32)
    lane = lax.broadcasted_iota(I32, tail.shape, 1)
    for g in range(width // group):
        part = value[:, g * group : (g + 1) * group]
        code = scale_code(jnp.max(jnp.abs(part), axis=1, keepdims=True))
        out_ref[at, :, start + g * group : start + (g + 1) * group] = to_code(part, code)
        tail = jnp.where(lane == g, code, tail)
    tail = jnp.where(lane == COUNT_LANE, count, tail)
    out_ref[at, :, start + width : start + width + LANES] = tail.astype(I32).astype(I16)


def decode_rows(ref, at, width, start=0):
    group = min(512, width)
    tail = ref[at, :, start + width : start + width + LANES].astype(I32).astype(F32)
    parts = []
    for g in range(width // group):
        level = ref[at, :, start + g * group : start + (g + 1) * group].astype(I32).astype(F32)
        parts.append(level * jnp.exp2(tail[:, g : g + 1] * (1.0 / STEPS)))
    return jnp.concatenate(parts, axis=1), tail[:, COUNT_LANE : COUNT_LANE + 1]


def table_kernel(blocks, terms, slots, place, v_ref, *refs):
    ranks, (send_ref, keep_ref, table) = refs[:terms], refs[terms:]
    rank_total = ranks[0][...]
    for term in ranks[1:]:
        rank_total = rank_total + term[...]
    high, low = split(rank_total)
    rank = rank_total.shape[0]
    width = v_ref.shape[1]
    length = v_ref.shape[0] // blocks
    table[...] = jnp.zeros_like(table)
    both = jnp.concatenate([high, low], axis=0)
    for b in range(blocks):
        cut = slice(b * length, (b + 1) * length)
        outer = jnp.dot(both[:, cut], v_ref[cut], preferred_element_type=F32)
        table[place[b]] += outer[:rank] + outer[rank:]
    for m in range(slots):
        count = jnp.int32(0)
        for b in range(blocks):
            count += (place[b] == m).astype(I32)
        count = count.astype(F32)
        if m % 2:
            encode_rows(table[m], count, send_ref, m // 2)
        else:
            keep_ref[m // 2, :, :width] = table[m]
            keep_ref[m // 2, :, width:] = jnp.full((rank, LANES), count, F32)


def table_sums(place, v, ranks, blocks, slots):
    rows, width = v.shape
    rank = ranks[0].shape[0]
    half = slots // 2
    return pl.pallas_call(
        functools.partial(table_kernel, blocks, len(ranks), slots),
        in_specs=[pl.BlockSpec(memory_space=pltpu.SMEM)] + whole(1 + len(ranks)),
        out_specs=whole(2),
        out_shape=[
            jax.ShapeDtypeStruct((half, rank, width + LANES), I16),
            jax.ShapeDtypeStruct((half, rank, width + LANES), F32),
        ],
        scratch_shapes=[VM((slots, rank, width), F32)],
        compiler_params=params(10),
        cost_estimate=cost(0, 0),
        name="table_sums",
    )(place, v, *ranks)


def combine_kernel(tables, *refs):
    keeps, gots, (own_ref, *sends) = refs[:tables], refs[tables : 2 * tables], refs[2 * tables :]
    start = 0
    for keep_ref, got_ref in zip(keeps, gots):
        wide = keep_ref.shape[2]
        width = wide - LANES
        for j in range(keep_ref.shape[0]):
            value, count = decode_rows(got_ref, j, width)
            value = value + keep_ref[j, :, :width]
            count = count + keep_ref[j, :, width : width + 1]
            if j == 0:
                own_ref[0, :, start : start + width] = value
                own_ref[0, :, start + width : start + wide] = jnp.broadcast_to(count, (count.shape[0], LANES))
            else:
                encode_rows(value, count, sends[j - 1], 0, start)
        start += wide


def combine(keeps, gots):
    half, rank, _ = keeps[0].shape
    wide = sum(k.shape[2] for k in keeps)
    return pl.pallas_call(
        functools.partial(combine_kernel, len(keeps)),
        in_specs=whole(2 * len(keeps)),
        out_specs=whole(half),
        out_shape=[jax.ShapeDtypeStruct((1, rank, wide), F32)]
        + [jax.ShapeDtypeStruct((1, rank, wide), I16)] * (half - 1),
        compiler_params=params(4),
        cost_estimate=cost(0, 0),
        name="combine",
    )(*keeps, *gots)


def finish_kernel(block_length, tables, own_ref, *refs):
    gots, outs = refs[:-tables], refs[-tables:]
    start = 0
    for out_ref in outs:
        width = out_ref.shape[2]
        value = own_ref[0, :, start : start + width]
        count = own_ref[0, :, start + width : start + width + 1]
        for got in gots:
            more, further = decode_rows(got, 0, width, start)
            value, count = value + more, count + further
        out_ref[0] = value * (2.0 / jnp.maximum(count * float(block_length), 1.0))
        start += width + LANES


def finish(own, gots, block_length, widths):
    _, rank, wide = own.shape
    return pl.pallas_call(
        functools.partial(finish_kernel, block_length, len(widths)),
        in_specs=whole(1 + len(gots)),
        out_specs=whole(len(widths)),
        out_shape=[jax.ShapeDtypeStruct((1, rank, width), F32) for width in widths],
        compiler_params=params(4),
        cost_estimate=cost(0, 0),
        name="finish",
    )(own, *gots)


def low_rank(both, maps):
    return lax.dot_general(both, jnp.concatenate([maps, maps], axis=0), TN, preferred_element_type=F32)


def through_kernel(blocks, cots, terms, pieces, first, order, place, *refs):
    cot_refs, refs = refs[:cots], refs[cots:]
    w_ref, refs = refs[0], refs[1:]
    ranks, refs = refs[:terms], refs[terms:]
    maps, (out_ref, table) = refs[:pieces], refs[-2:]
    gather_pieces(maps, table)
    rank_total = ranks[0][...]
    for term in ranks[1:]:
        rank_total = rank_total + term[...]
    both = jnp.concatenate(split(2.0 * rank_total), axis=0)
    width = cot_refs[0].shape[1]
    block = out_ref.shape[1]
    here = pl.ds(pl.multiple_of((first + pl.program_id(0)) * block, block), block)
    length = cot_refs[0].shape[0] // blocks
    total = None
    for i, cot in enumerate(cot_refs):
        columns = pl.ds(pl.multiple_of(order[i] * width, width), width)
        term = lax.dot_general(cot[...], w_ref[here, columns], NT, preferred_element_type=F32)
        total = term if total is None else total + term
    for b in range(blocks):
        cut = slice(b * length, (b + 1) * length)
        out_ref[cut] = total[cut] + low_rank(both[:, cut], table[place[b]])


def through(order, place, cots, w, ranks, maps, blocks, part, parts, before=()):
    rows, width = cots[0].shape
    depth, features = w.shape
    count = sum(m.shape[0] for m in maps)
    rank = maps[0].shape[1]
    block = min(512, depth // parts)
    steps = depth // parts // block
    first = part * steps
    operands = [*cots, w, *ranks, *maps, *before]
    return pl.pallas_call(
        functools.partial(through_kernel, blocks, len(cots), len(ranks), len(maps), first),
        grid_spec=pltpu.PrefetchScalarGridSpec(
            num_scalar_prefetch=2,
            grid=(steps,),
            in_specs=[pl.BlockSpec((rows, width), lambda i, *_: (0, 0)) for _ in cots]
            + whole(1)
            + [pl.BlockSpec((rank, rows), lambda i, *_: (0, 0)) for _ in ranks]
            + [pl.BlockSpec((m.shape[0], rank, block), lambda i, *_: (0, 0, first + i)) for m in maps]
            + [pl.BlockSpec(memory_space=pl.ANY) for _ in before],
            out_specs=pl.BlockSpec((rows, block), lambda i, *_: (0, first + i)),
            scratch_shapes=[VM((count, rank, block), BF16)],
        ),
        out_shape=jax.ShapeDtypeStruct((rows, depth), F32),
        input_output_aliases={1 + len(operands): 0} if before else {},
        compiler_params=params(16, 1),
        cost_estimate=cost(0, 0),
        name="through",
    )(order, place, *operands)


def project_kernel(blocks, group, codes, terms, pieces, place, own_ref, *refs):
    code_refs, refs = refs[:codes], refs[codes:]
    ranks, refs = refs[:terms], refs[terms:]
    maps, (out_ref, table) = refs[:pieces], refs[pieces:]
    gather_pieces(maps, table)
    rank_total = ranks[0][...]
    for term in ranks[1:]:
        rank_total = rank_total + term[...]
    both = jnp.concatenate(split(2.0 * rank_total), axis=0)
    rows = own_ref.shape[0]
    length = rows // blocks
    for b in range(blocks):
        cut = slice(b * length, (b + 1) * length)
        total = own_ref[cut] + low_rank(both[:, cut], table[place[b]])
        for code in code_refs:
            g = b * length // group
            scale = jnp.exp2(code[0, rows : rows + 16].astype(I32).astype(F32) * (1.0 / STEPS))
            total = total + code[0, cut].astype(I32).astype(F32) * scale[g : g + 1]
        out_ref[cut] = total


def project(place, own, codes, ranks, maps, blocks, group):
    rows, width = own.shape
    count = sum(m.shape[0] for m in maps)
    rank = maps[0].shape[1]
    return pl.pallas_call(
        functools.partial(project_kernel, blocks, group, len(codes), len(ranks), len(maps)),
        in_specs=[pl.BlockSpec(memory_space=pltpu.SMEM)] + whole(1 + len(codes) + len(ranks) + len(maps)),
        out_specs=whole(1)[0],
        out_shape=jax.ShapeDtypeStruct((rows, width), F32),
        scratch_shapes=[VM((count, rank, width), BF16)],
        compiler_params=params(8),
        cost_estimate=cost(0, 0),
        name="project",
    )(place, own, *codes, *ranks, *maps)


def swap(value, axis, size, mask):
    return lax.ppermute(value, axis, [(i, i ^ mask) for i in range(size)])


def after(value, earlier):
    return lax.optimization_barrier((value, earlier))[0]


def shards(reps, tps, tokens, weight, cot, maps_in, maps_out, tenant, slot_of):
    chips = tps // 2
    blocks = tenant.shape[0]
    rows = tokens.shape[0]
    length = rows // blocks
    slots = reps
    width = cot.shape[1]
    rep, tp = lax.axis_index("rep"), lax.axis_index("tp")
    core = functools.partial(swap, axis="tp", size=tps, mask=1)

    def over_y(value, k):
        return swap(value, "tp", tps, 2 * k)

    def over_rep(value, mask):
        return swap(value, "rep", reps, mask)

    peers = range(1, chips)

    bits = [reps >> i for i in range(1, reps.bit_length())]
    out_held, in_held = maps_out, maps_in
    out_got = over_rep(out_held, bits[0])
    in_got = over_rep(in_held, bits[0])
    cot_y = [over_y(cot, k) for k in peers]
    place, order = plan(rep, tp, tenant, slot_of, tps)
    out_got = after(out_got, place)
    in_gots = [in_got]
    for bit in bits[1:]:
        out_held = jnp.concatenate([out_held, out_got], axis=0)
        out_got = over_rep(out_held, bit)
    for bit in bits[1:]:
        in_held = jnp.concatenate([in_held, in_gots[-1]], axis=0)
        in_gots.append(over_rep(in_held, bit))
    outs_all, ins_all = [out_held, out_got], [in_held, in_gots[-1]]

    def spread(chip_sum):
        return [chip_sum] + [over_y(chip_sum, k) for k in peers]

    back_part = rank_part(place, after(cot, in_gots[0]), outs_all, blocks)
    back_sum = back_part + core(back_part)
    back = spread(back_sum)
    sent_peer = base_send(
        order, after(tokens, (back_sum, cot_y, in_gots[1])), weight, [2 * k + 1 for k in peers], width
    )
    in_send, in_keep = table_sums(place, after(tokens, sent_peer), back, blocks, slots)
    in_swapped = over_rep(in_send, 1)

    got_peer = core(after(sent_peer, in_send))
    sent_own = base_send(order, after(tokens, in_send), weight, [1], width)
    forward_part = rank_part(place, after(tokens, sent_own), ins_all, blocks)
    codes = base_code(order, after(tokens, forward_part), weight, got_peer, [2 * k for k in peers], 128)
    forward_sum = forward_part + core(forward_part)
    forward = spread(forward_sum)
    got_own = core(after(sent_own, forward_sum))
    own_base = base_own(order, after(tokens, codes[0]), weight, got_own)
    cots = []
    for piece in [cot] + cot_y:
        cots += [piece, core(after(piece, codes[0]))]
    out_send, out_keep = table_sums(place, after(cot, own_base), forward, blocks, slots)
    out_swapped = over_rep(out_send, 1)
    base_codes = [over_y(after(codes[k - 1], forward), k) for k in peers]

    half = through(order, place, [after(cots[0], out_send)] + cots[1:], weight, back, ins_all, blocks, 0, 2)
    grads_own, *grads = combine([in_keep, out_keep], [in_swapped, after(out_swapped, half)])
    grads_got = [over_rep(g, 2 * (j + 1)) for j, g in enumerate(grads)]
    token_grad = through(
        order, place, [after(cots[0], grads_own)] + cots[1:], weight, back, ins_all, blocks, 1, 2, [half]
    )
    projected = project(place, after(own_base, token_grad), base_codes, forward, outs_all, blocks, 128)
    grad_in, grad_out = finish(after(grads_own, projected), grads_got, length, [tokens.shape[1], width])
    return projected, token_grad, grad_in, grad_out


def solution(mesh):
    placed = (
        P("rep", "tp"),
        P("tp", None),
        P("rep", "tp"),
        P("rep", None, "tp"),
        P("rep", None, "tp"),
        P("rep"),
        P(),
    )
    return jax.shard_map(
        functools.partial(shards, mesh.shape["rep"], mesh.shape["tp"]),
        mesh=mesh,
        in_specs=placed,
        out_specs=(P("rep", "tp"), P("rep", "tp"), P("rep", None, "tp"), P("rep", None, "tp")),
        check_vma=False,
    )
```

```python
import functools

import jax
import jax.numpy as jnp
from jax import lax
from jax.experimental import pallas as pl
from jax.experimental.pallas import tpu as pltpu
from jax.sharding import PartitionSpec as P

F32, BF16, I32, I16 = jnp.float32, jnp.bfloat16, jnp.int32, jnp.int16
VM = pltpu.VMEM
STEPS = 128.0
CODE_TOP = 32767.0
LEAST = 1e-33
LANES = 128
COUNT_LANE = 64
WORK = 30e9
NT = (((1,), (1,)), ((), ()))
TN = (((0,), (0,)), ((), ()))


def params(mib, grid_dims=0):
    return pltpu.CompilerParams(
        vmem_limit_bytes=mib << 20,
        dimension_semantics=("arbitrary",) * grid_dims if grid_dims else None,
    )


def cost(flops, moved):
    return pl.CostEstimate(flops=int(flops), bytes_accessed=int(moved), transcendentals=0)


def whole(n):
    return [pl.BlockSpec(memory_space=VM)] * n


def scale_code(top):
    return jnp.ceil(STEPS * (jnp.log2(jnp.maximum(top, LEAST)) - 15.0)) + 1.0


def to_code(value, code):
    level = jnp.round(value * jnp.exp2(code * (-1.0 / STEPS)))
    return jnp.clip(level, -CODE_TOP, CODE_TOP).astype(I32).astype(I16)


def from_code(level, code):
    return level.astype(I32).astype(F32) * jnp.exp2(code.astype(I32).astype(F32) * (1.0 / STEPS))


def split(value):
    high = value.astype(BF16)
    return high, (value - high.astype(F32)).astype(BF16)


def plan_kernel(ids, tenant, slot_of, place, order):
    for b in range(place.shape[0]):
        place[b] = jnp.bitwise_xor(slot_of[tenant[b]], ids[0])
    for i in range(order.shape[0]):
        order[i] = jnp.bitwise_xor(ids[1], i)


def plan(rep, tp, tenant, slot_of, tps):
    smem = pl.BlockSpec(memory_space=pltpu.SMEM)
    ids = jnp.stack([rep, tp]).astype(I32)
    return pl.pallas_call(
        plan_kernel,
        in_specs=[smem] * 3,
        out_specs=[smem] * 2,
        out_shape=[jax.ShapeDtypeStruct(tenant.shape, I32), jax.ShapeDtypeStruct((tps,), I32)],
        compiler_params=params(16),
        cost_estimate=cost(WORK, 0),
        name="plan",
    )(ids, tenant, slot_of)


def base_send_kernel(masks, order, x_ref, w_ref, out_ref):
    width = out_ref.shape[2]
    for i, mask in enumerate(masks):
        columns = pl.ds(pl.multiple_of(order[mask] * width, width), width)
        out_ref[i] = jnp.dot(x_ref[...], w_ref[:, columns], preferred_element_type=F32)


def base_send(order, x, w, masks, width):
    rows, depth = x.shape
    return pl.pallas_call(
        functools.partial(base_send_kernel, masks),
        in_specs=[pl.BlockSpec(memory_space=pltpu.SMEM)] + whole(2),
        out_specs=whole(1)[0],
        out_shape=jax.ShapeDtypeStruct((len(masks), rows, width), F32),
        compiler_params=params(16),
        cost_estimate=cost(0, 0),
        name="base_send",
    )(order, x, w)


def base_own_kernel(order, x_ref, w_ref, got_ref, own_ref):
    width = own_ref.shape[1]
    columns = pl.ds(pl.multiple_of(order[0] * width, width), width)
    own_ref[...] = got_ref[0] + jnp.dot(x_ref[...], w_ref[:, columns], preferred_element_type=F32)


def base_own(order, x, w, got):
    _, rows, width = got.shape
    return pl.pallas_call(
        base_own_kernel,
        in_specs=[pl.BlockSpec(memory_space=pltpu.SMEM)] + whole(3),
        out_specs=whole(1)[0],
        out_shape=jax.ShapeDtypeStruct((rows, width), F32),
        compiler_params=params(16),
        cost_estimate=cost(WORK, 0),
        name="base_own",
    )(order, x, w, got)


def base_code_kernel(group, masks, order, x_ref, w_ref, got_ref, *code_refs):
    rows, width = got_ref.shape[1:]
    block = min(256, width)
    for i, (mask, code_ref) in enumerate(zip(masks, code_refs)):
        for j in range(width // block):
            cut = slice(j * block, (j + 1) * block)
            columns = pl.ds(pl.multiple_of(order[mask] * width + j * block, block), block)
            total = got_ref[i, :, cut] + jnp.dot(x_ref[...], w_ref[:, columns], preferred_element_type=F32)
            tail = jnp.zeros((16, block), F32)
            row = lax.broadcasted_iota(I32, tail.shape, 0)
            for g in range(rows // group):
                part = total[g * group : (g + 1) * group]
                code = scale_code(jnp.max(jnp.abs(part), axis=0, keepdims=True))
                code_ref[0, g * group : (g + 1) * group, cut] = to_code(part, code)
                tail = jnp.where(row == g, code, tail)
            code_ref[0, rows:, cut] = tail.astype(I32).astype(I16)


def base_code(order, x, w, got, masks, group):
    count, rows, width = got.shape
    return pl.pallas_call(
        functools.partial(base_code_kernel, group, masks),
        in_specs=[pl.BlockSpec(memory_space=pltpu.SMEM)] + whole(3),
        out_specs=whole(count),
        out_shape=[jax.ShapeDtypeStruct((1, rows + 16, width), I16)] * count,
        compiler_params=params(16),
        cost_estimate=cost(0, 0),
        name="base_code",
    )(order, x, w, got)


def gather_masks(count):
    masks, bit = [0], count // 2
    while bit:
        masks, bit = masks + [m ^ bit for m in masks], bit // 2
    return masks


def gather_pieces(pieces, table):
    masks = iter(gather_masks(table.shape[0]))
    for piece in pieces:
        for i in range(piece.shape[0]):
            table[next(masks)] = piece[i]


def rank_kernel(blocks, pieces, place, v_ref, *refs):
    maps, out_ref, table = refs[:pieces], refs[pieces], refs[pieces + 1]
    gather_pieces(maps, table)
    length = v_ref.shape[0] // blocks
    for b in range(blocks):
        out_ref[:, b * length : (b + 1) * length] = lax.dot_general(
            table[place[b]], v_ref[b * length : (b + 1) * length], NT, preferred_element_type=F32
        )


def rank_part(place, v, maps, blocks):
    rows, width = v.shape
    count = sum(m.shape[0] for m in maps)
    rank = maps[0].shape[1]
    return pl.pallas_call(
        functools.partial(rank_kernel, blocks, len(maps)),
        in_specs=[pl.BlockSpec(memory_space=pltpu.SMEM)] + whole(1 + len(maps)),
        out_specs=whole(1)[0],
        out_shape=jax.ShapeDtypeStruct((rank, rows), F32),
        scratch_shapes=[VM((count, rank, width), BF16)],
        compiler_params=params(16),
        cost_estimate=cost(WORK, 0),
        name="rank_part",
    )(place, v, *maps)


def encode_rows(value, count, out_ref, at, start=0):
    rank, width = value.shape
    group = min(512, width)
    tail = jnp.zeros((rank, LANES), F32)
    lane = lax.broadcasted_iota(I32, tail.shape, 1)
    for g in range(width // group):
        part = value[:, g * group : (g + 1) * group]
        code = scale_code(jnp.max(jnp.abs(part), axis=1, keepdims=True))
        out_ref[at, :, start + g * group : start + (g + 1) * group] = to_code(part, code)
        tail = jnp.where(lane == g, code, tail)
    tail = jnp.where(lane == COUNT_LANE, count, tail)
    out_ref[at, :, start + width : start + width + LANES] = tail.astype(I32).astype(I16)


def decode_rows(ref, at, width, start=0):
    group = min(512, width)
    tail = ref[at, :, start + width : start + width + LANES].astype(I32).astype(F32)
    parts = []
    for g in range(width // group):
        level = ref[at, :, start + g * group : start + (g + 1) * group].astype(I32).astype(F32)
        parts.append(level * jnp.exp2(tail[:, g : g + 1] * (1.0 / STEPS)))
    return jnp.concatenate(parts, axis=1), tail[:, COUNT_LANE : COUNT_LANE + 1]


def table_kernel(blocks, terms, slots, place, v_ref, *refs):
    ranks, (send_ref, keep_ref, table) = refs[:terms], refs[terms:]
    rank_total = ranks[0][...]
    for term in ranks[1:]:
        rank_total = rank_total + term[...]
    high, low = split(rank_total)
    rank = rank_total.shape[0]
    width = v_ref.shape[1]
    length = v_ref.shape[0] // blocks
    table[...] = jnp.zeros_like(table)
    both = jnp.concatenate([high, low], axis=0)
    for b in range(blocks):
        cut = slice(b * length, (b + 1) * length)
        outer = jnp.dot(both[:, cut], v_ref[cut], preferred_element_type=F32)
        table[place[b]] += outer[:rank] + outer[rank:]
    for m in range(slots):
        count = jnp.int32(0)
        for b in range(blocks):
            count += (place[b] == m).astype(I32)
        count = count.astype(F32)
        if m % 2:
            encode_rows(table[m], count, send_ref, m // 2)
        else:
            keep_ref[m // 2, :, :width] = table[m]
            keep_ref[m // 2, :, width:] = jnp.full((rank, LANES), count, F32)


def table_sums(place, v, ranks, blocks, slots):
    rows, width = v.shape
    rank = ranks[0].shape[0]
    half = slots // 2
    return pl.pallas_call(
        functools.partial(table_kernel, blocks, len(ranks), slots),
        in_specs=[pl.BlockSpec(memory_space=pltpu.SMEM)] + whole(1 + len(ranks)),
        out_specs=whole(2),
        out_shape=[
            jax.ShapeDtypeStruct((half, rank, width + LANES), I16),
            jax.ShapeDtypeStruct((half, rank, width + LANES), F32),
        ],
        scratch_shapes=[VM((slots, rank, width), F32)],
        compiler_params=params(16),
        cost_estimate=cost(WORK, 0),
        name="table_sums",
    )(place, v, *ranks)


def combine_kernel(tables, *refs):
    keeps, gots, (own_ref, *sends) = refs[:tables], refs[tables : 2 * tables], refs[2 * tables :]
    start = 0
    for keep_ref, got_ref in zip(keeps, gots):
        wide = keep_ref.shape[2]
        width = wide - LANES
        for j in range(keep_ref.shape[0]):
            value, count = decode_rows(got_ref, j, width)
            value = value + keep_ref[j, :, :width]
            count = count + keep_ref[j, :, width : width + 1]
            if j == 0:
                own_ref[0, :, start : start + width] = value
                own_ref[0, :, start + width : start + wide] = jnp.broadcast_to(count, (count.shape[0], LANES))
            else:
                encode_rows(value, count, sends[j - 1], 0, start)
        start += wide


def combine(keeps, gots):
    half, rank, _ = keeps[0].shape
    wide = sum(k.shape[2] for k in keeps)
    return pl.pallas_call(
        functools.partial(combine_kernel, len(keeps)),
        in_specs=whole(2 * len(keeps)),
        out_specs=whole(half),
        out_shape=[jax.ShapeDtypeStruct((1, rank, wide), F32)]
        + [jax.ShapeDtypeStruct((1, rank, wide), I16)] * (half - 1),
        compiler_params=params(16),
        cost_estimate=cost(WORK, 0),
        name="combine",
    )(*keeps, *gots)


def finish_kernel(block_length, tables, own_ref, *refs):
    gots, outs = refs[:-tables], refs[-tables:]
    start = 0
    for out_ref in outs:
        width = out_ref.shape[2]
        value = own_ref[0, :, start : start + width]
        count = own_ref[0, :, start + width : start + width + 1]
        for got in gots:
            more, further = decode_rows(got, 0, width, start)
            value, count = value + more, count + further
        out_ref[0] = value * (2.0 / jnp.maximum(count * float(block_length), 1.0))
        start += width + LANES


def finish(own, gots, block_length, widths):
    _, rank, wide = own.shape
    return pl.pallas_call(
        functools.partial(finish_kernel, block_length, len(widths)),
        in_specs=whole(1 + len(gots)),
        out_specs=whole(len(widths)),
        out_shape=[jax.ShapeDtypeStruct((1, rank, width), F32) for width in widths],
        compiler_params=params(16),
        cost_estimate=cost(WORK, 0),
        name="finish",
    )(own, *gots)


def low_rank(both, maps):
    return lax.dot_general(both, jnp.concatenate([maps, maps], axis=0), TN, preferred_element_type=F32)


def through_kernel(blocks, cots, terms, pieces, first, order, place, *refs):
    cot_refs, refs = refs[:cots], refs[cots:]
    w_ref, refs = refs[0], refs[1:]
    ranks, refs = refs[:terms], refs[terms:]
    maps, (out_ref, table) = refs[:pieces], refs[-2:]
    gather_pieces(maps, table)
    rank_total = ranks[0][...]
    for term in ranks[1:]:
        rank_total = rank_total + term[...]
    both = jnp.concatenate(split(2.0 * rank_total), axis=0)
    width = cot_refs[0].shape[1]
    block = out_ref.shape[1]
    here = pl.ds(pl.multiple_of((first + pl.program_id(0)) * block, block), block)
    length = cot_refs[0].shape[0] // blocks
    total = None
    for i, cot in enumerate(cot_refs):
        columns = pl.ds(pl.multiple_of(order[i] * width, width), width)
        term = lax.dot_general(cot[...], w_ref[here, columns], NT, preferred_element_type=F32)
        total = term if total is None else total + term
    for b in range(blocks):
        cut = slice(b * length, (b + 1) * length)
        out_ref[cut] = total[cut] + low_rank(both[:, cut], table[place[b]])


def through(order, place, cots, w, ranks, maps, blocks, part, parts, before=()):
    rows, width = cots[0].shape
    depth, features = w.shape
    count = sum(m.shape[0] for m in maps)
    rank = maps[0].shape[1]
    block = min(512, depth // parts)
    steps = depth // parts // block
    first = part * steps
    operands = [*cots, w, *ranks, *maps, *before]
    return pl.pallas_call(
        functools.partial(through_kernel, blocks, len(cots), len(ranks), len(maps), first),
        grid_spec=pltpu.PrefetchScalarGridSpec(
            num_scalar_prefetch=2,
            grid=(steps,),
            in_specs=[pl.BlockSpec((rows, width), lambda i, *_: (0, 0)) for _ in cots]
            + whole(1)
            + [pl.BlockSpec((rank, rows), lambda i, *_: (0, 0)) for _ in ranks]
            + [pl.BlockSpec((m.shape[0], rank, block), lambda i, *_: (0, 0, first + i)) for m in maps]
            + [pl.BlockSpec(memory_space=pl.ANY) for _ in before],
            out_specs=pl.BlockSpec((rows, block), lambda i, *_: (0, first + i)),
            scratch_shapes=[VM((count, rank, block), BF16)],
        ),
        out_shape=jax.ShapeDtypeStruct((rows, depth), F32),
        input_output_aliases={1 + len(operands): 0} if before else {},
        compiler_params=params(16, 1),
        cost_estimate=cost(WORK, 0),
        name="through",
    )(order, place, *operands)


def project_kernel(blocks, group, codes, terms, pieces, place, own_ref, *refs):
    code_refs, refs = refs[:codes], refs[codes:]
    ranks, refs = refs[:terms], refs[terms:]
    maps, (out_ref, table) = refs[:pieces], refs[pieces:]
    gather_pieces(maps, table)
    rank_total = ranks[0][...]
    for term in ranks[1:]:
        rank_total = rank_total + term[...]
    both = jnp.concatenate(split(2.0 * rank_total), axis=0)
    rows = own_ref.shape[0]
    length = rows // blocks
    for b in range(blocks):
        cut = slice(b * length, (b + 1) * length)
        total = own_ref[cut] + low_rank(both[:, cut], table[place[b]])
        for code in code_refs:
            g = b * length // group
            scale = jnp.exp2(code[0, rows : rows + 16].astype(I32).astype(F32) * (1.0 / STEPS))
            total = total + code[0, cut].astype(I32).astype(F32) * scale[g : g + 1]
        out_ref[cut] = total


def project(place, own, codes, ranks, maps, blocks, group):
    rows, width = own.shape
    count = sum(m.shape[0] for m in maps)
    rank = maps[0].shape[1]
    return pl.pallas_call(
        functools.partial(project_kernel, blocks, group, len(codes), len(ranks), len(maps)),
        in_specs=[pl.BlockSpec(memory_space=pltpu.SMEM)] + whole(1 + len(codes) + len(ranks) + len(maps)),
        out_specs=whole(1)[0],
        out_shape=jax.ShapeDtypeStruct((rows, width), F32),
        scratch_shapes=[VM((count, rank, width), BF16)],
        compiler_params=params(16),
        cost_estimate=cost(0, 0),
        name="project",
    )(place, own, *codes, *ranks, *maps)


def swap(value, axis, size, mask):
    return lax.ppermute(value, axis, [(i, i ^ mask) for i in range(size)])


def after(value, earlier):
    return lax.optimization_barrier((value, earlier))[0]


def shards(reps, tps, tokens, weight, cot, maps_in, maps_out, tenant, slot_of):
    chips = tps // 2
    blocks = tenant.shape[0]
    length = tokens.shape[0] // blocks
    slots = reps
    width = cot.shape[1]
    rep, tp = lax.axis_index("rep"), lax.axis_index("tp")
    core = functools.partial(swap, axis="tp", size=tps, mask=1)

    def over_y(value, k):
        return swap(value, "tp", tps, 2 * k)

    def over_rep(value, mask):
        return swap(value, "rep", reps, mask)

    def spread(chip_sum):
        return [chip_sum] + [over_y(chip_sum, k) for k in peers]

    peers = range(1, chips)
    bits = [reps >> i for i in range(1, reps.bit_length())]
    out_held, in_held = maps_out, maps_in
    out_got = over_rep(out_held, bits[0])
    in_got = over_rep(in_held, bits[0])
    cot_y = [over_y(cot, k) for k in peers]
    place, order = plan(rep, tp, tenant, slot_of, tps)
    out_got = after(out_got, place)
    for bit in bits[1:]:
        out_held = jnp.concatenate([out_held, out_got], axis=0)
        in_held = jnp.concatenate([in_held, in_got], axis=0)
        if bit == 1:
            out_held, in_held = after((out_held, in_held), sent_peer)
        out_held, in_held = lax.optimization_barrier((out_held, in_held))
        out_got, in_got = over_rep(out_held, bit), over_rep(in_held, bit)
        if bit == bits[1]:
            sent_peer = base_send(order, after(tokens, out_got), weight, [2 * k + 1 for k in peers], width)
    outs_all, ins_all = [out_held, out_got], [in_held, in_got]

    sent_own = base_send(order, after(tokens, out_held), weight, [1], width)
    got_peer, got_own = core(sent_peer), core(sent_own)
    back_part = rank_part(place, after(cot, (cot_y, sent_own)), outs_all, blocks)
    back_sum = back_part + core(back_part)
    back = spread(back_sum)
    codes = base_code(order, after(tokens, back_sum), weight, got_peer, [2 * k for k in peers], 128)
    forward_part = rank_part(place, after(tokens, codes[0]), ins_all, blocks)
    in_send, in_keep = table_sums(place, after(tokens, forward_part), back, blocks, slots)
    in_swapped = over_rep(in_send, 1)
    forward_sum = forward_part + after(core(forward_part), in_send)
    forward = spread(forward_sum)
    base_codes = [over_y(after(codes[k - 1], forward_sum), k) for k in peers]
    cots = []
    for piece in [cot] + cot_y:
        cots += [piece, core(after(piece, back_sum))]
    half = through(order, place, [after(cots[0], forward_sum)] + cots[1:], weight, back, ins_all, blocks, 0, 2)
    out_send, out_keep = table_sums(place, after(cot, half), forward, blocks, slots)
    out_swapped = over_rep(out_send, 1)
    own_base = base_own(order, after(tokens, out_send), weight, got_own)
    grads_own, *grads = combine([in_keep, out_keep], [in_swapped, after(out_swapped, own_base)])
    grads_got = [over_rep(g, 2 * (j + 1)) for j, g in enumerate(grads)]
    token_grad = through(
        order, place, [after(cots[0], grads_own)] + cots[1:], weight, back, ins_all, blocks, 1, 2, [half]
    )
    projected = project(place, after(own_base, token_grad), base_codes, forward, outs_all, blocks, 128)
    grad_in, grad_out = finish(after(grads_own, projected), grads_got, length, [tokens.shape[1], width])
    return projected, token_grad, grad_in, grad_out


def solution(mesh):
    placed = (
        P("rep", "tp"),
        P("tp", None),
        P("rep", "tp"),
        P("rep", None, "tp"),
        P("rep", None, "tp"),
        P("rep"),
        P(),
    )
    return jax.shard_map(
        functools.partial(shards, mesh.shape["rep"], mesh.shape["tp"]),
        mesh=mesh,
        in_specs=placed,
        out_specs=(P("rep", "tp"), P("rep", "tp"), P("rep", None, "tp"), P("rep", None, "tp")),
        check_vma=False,
    )
```

```python
import functools

import jax
import jax.numpy as jnp
from jax import lax
from jax.experimental import pallas as pl
from jax.experimental.pallas import tpu as pltpu
from jax.sharding import PartitionSpec as P

F32, BF16, I32, I16 = jnp.float32, jnp.bfloat16, jnp.int32, jnp.int16
VM = pltpu.VMEM
STEPS = 128.0
CODE_TOP = 32767.0
LEAST = 1e-33
LANES = 128
COUNT_LANE = 64
WORK = 10e9
NT = (((1,), (1,)), ((), ()))
TN = (((0,), (0,)), ((), ()))


def params(mib, grid_dims=0):
    return pltpu.CompilerParams(
        vmem_limit_bytes=mib << 20,
        dimension_semantics=("arbitrary",) * grid_dims if grid_dims else None,
    )


def cost(flops, moved):
    return pl.CostEstimate(flops=int(flops), bytes_accessed=int(moved), transcendentals=0)


def whole(n):
    return [pl.BlockSpec(memory_space=VM)] * n


def scale_code(top):
    return jnp.ceil(STEPS * (jnp.log2(jnp.maximum(top, LEAST)) - 15.0)) + 1.0


def to_code(value, code):
    level = jnp.round(value * jnp.exp2(code * (-1.0 / STEPS)))
    return jnp.clip(level, -CODE_TOP, CODE_TOP).astype(I32).astype(I16)


def from_code(level, code):
    return level.astype(I32).astype(F32) * jnp.exp2(code.astype(I32).astype(F32) * (1.0 / STEPS))


def split(value):
    high = value.astype(BF16)
    return high, (value - high.astype(F32)).astype(BF16)


def plan_kernel(rep, tenant, slot_of, place):
    blocks = tenant.shape[0]
    length = place.shape[1] // blocks
    for b in range(blocks):
        mask = jnp.bitwise_xor(slot_of[tenant[b]], rep[0])
        place[:, b * length : (b + 1) * length] = jnp.full((1, length), mask, I32)


def plan(rep, tenant, slot_of, rows):
    smem = pl.BlockSpec(memory_space=pltpu.SMEM)
    return pl.pallas_call(
        plan_kernel,
        in_specs=[smem] * 3,
        out_specs=whole(1)[0],
        out_shape=jax.ShapeDtypeStruct((1, rows), I32),
        compiler_params=params(16),
        cost_estimate=cost(WORK, 0),
        name="plan",
    )(jnp.stack([rep, rep]).astype(I32), tenant, slot_of)


def owner(mask):
    return jnp.bitwise_xor(lax.axis_index("tp"), mask)


def base_send_kernel(masks, x_ref, w_ref, out_ref):
    width = out_ref.shape[2]
    for i, mask in enumerate(masks):
        columns = pl.ds(pl.multiple_of(owner(mask) * width, width), width)
        out_ref[i] = jnp.dot(x_ref[...], w_ref[:, columns], preferred_element_type=F32)


def base_send(x, w, masks, width):
    rows, depth = x.shape
    return pl.pallas_call(
        functools.partial(base_send_kernel, masks),
        in_specs=whole(2),
        out_specs=whole(1)[0],
        out_shape=jax.ShapeDtypeStruct((len(masks), rows, width), F32),
        compiler_params=params(16),
        cost_estimate=cost(0, 0),
        name="base_send",
    )(x, w)


def base_own_kernel(x_ref, w_ref, got_ref, own_ref):
    width = own_ref.shape[1]
    columns = pl.ds(pl.multiple_of(owner(0) * width, width), width)
    own_ref[...] = got_ref[0] + jnp.dot(x_ref[...], w_ref[:, columns], preferred_element_type=F32)


def base_own(x, w, got):
    _, rows, width = got.shape
    return pl.pallas_call(
        base_own_kernel,
        in_specs=whole(3),
        out_specs=whole(1)[0],
        out_shape=jax.ShapeDtypeStruct((rows, width), F32),
        compiler_params=params(16),
        cost_estimate=cost(0, 0),
        name="base_own",
    )(x, w, got)


def base_code_kernel(group, masks, x_ref, w_ref, got_ref, *code_refs):
    rows, width = got_ref.shape[1:]
    block = min(256, width)
    for i, (mask, code_ref) in enumerate(zip(masks, code_refs)):
        for j in range(width // block):
            cut = slice(j * block, (j + 1) * block)
            columns = pl.ds(pl.multiple_of(owner(mask) * width + j * block, block), block)
            total = got_ref[i, :, cut] + jnp.dot(x_ref[...], w_ref[:, columns], preferred_element_type=F32)
            tail = jnp.zeros((16, block), F32)
            row = lax.broadcasted_iota(I32, tail.shape, 0)
            for g in range(rows // group):
                part = total[g * group : (g + 1) * group]
                code = scale_code(jnp.max(jnp.abs(part), axis=0, keepdims=True))
                code_ref[0, g * group : (g + 1) * group, cut] = to_code(part, code)
                tail = jnp.where(row == g, code, tail)
            code_ref[0, rows:, cut] = tail.astype(I32).astype(I16)


def base_code(x, w, got, masks, group):
    count, rows, width = got.shape
    return pl.pallas_call(
        functools.partial(base_code_kernel, group, masks),
        in_specs=whole(3),
        out_specs=whole(count),
        out_shape=[jax.ShapeDtypeStruct((1, rows + 16, width), I16)] * count,
        compiler_params=params(16),
        cost_estimate=cost(0, 0),
        name="base_code",
    )(x, w, got)


def gather_masks(count):
    masks, bit = [0], count // 2
    while bit:
        masks, bit = masks + [m ^ bit for m in masks], bit // 2
    return masks


def stacked(pieces, here=slice(None)):
    return jnp.concatenate([p[:, :, here].reshape(p.shape[0] * p.shape[1], -1) for p in pieces], axis=0)


def spread_rows(value, place, masks):
    return jnp.concatenate([jnp.where(place == m, value, 0.0) for m in masks], axis=0)


def rank_total(ranks):
    total = ranks[0][...]
    for term in ranks[1:]:
        total = total + term[...]
    return total


def both_parts(total, place, masks):
    high, low = split(total)
    parts = [spread_rows(part.astype(F32), place, masks) for part in (high, low)]
    return jnp.concatenate(parts, axis=0)


def rank_kernel(place_ref, v_ref, *refs):
    maps, out_ref = refs[:-1], refs[-1]
    rank = out_ref.shape[0]
    every = lax.dot_general(stacked(maps), v_ref[...], NT, preferred_element_type=F32)
    place = place_ref[...]
    total = jnp.zeros(out_ref.shape, F32)
    for i, mask in enumerate(gather_masks(every.shape[0] // rank)):
        total = jnp.where(place == mask, every[i * rank : (i + 1) * rank], total)
    out_ref[...] = total


def rank_part(place, v, maps):
    rank = maps[0].shape[1]
    return pl.pallas_call(
        rank_kernel,
        in_specs=whole(2 + len(maps)),
        out_specs=whole(1)[0],
        out_shape=jax.ShapeDtypeStruct((rank, v.shape[0]), F32),
        compiler_params=params(16),
        cost_estimate=cost(WORK, 0),
        name="rank_part",
    )(place, v, *maps)


def encode_rows(value, count, out_ref, at, start=0):
    rank, width = value.shape
    group = min(512, width)
    tail = jnp.zeros((rank, LANES), F32)
    lane = lax.broadcasted_iota(I32, tail.shape, 1)
    for g in range(width // group):
        part = value[:, g * group : (g + 1) * group]
        code = scale_code(jnp.max(jnp.abs(part), axis=1, keepdims=True))
        out_ref[at, :, start + g * group : start + (g + 1) * group] = to_code(part, code)
        tail = jnp.where(lane == g, code, tail)
    tail = jnp.where(lane == COUNT_LANE, count, tail)
    out_ref[at, :, start + width : start + width + LANES] = tail.astype(I32).astype(I16)


def decode_rows(ref, at, width, start=0):
    group = min(512, width)
    tail = ref[at, :, start + width : start + width + LANES].astype(I32).astype(F32)
    parts = []
    for g in range(width // group):
        level = ref[at, :, start + g * group : start + (g + 1) * group].astype(I32).astype(F32)
        parts.append(level * jnp.exp2(tail[:, g : g + 1] * (1.0 / STEPS)))
    return jnp.concatenate(parts, axis=1), tail[:, COUNT_LANE : COUNT_LANE + 1]


def table_kernel(blocks, slots, place_ref, v_ref, *refs):
    ranks, (send_ref, keep_ref) = refs[:-2], refs[-2:]
    place = place_ref[...]
    rows, width = v_ref.shape
    rank = ranks[0].shape[0]
    factors = both_parts(rank_total(ranks), place, range(slots)).astype(BF16)
    group = min(512, width)
    lane = lax.broadcasted_iota(I32, (rank, LANES), 1)
    tails = {}
    for mask in range(slots):
        count = jnp.sum(jnp.where(place == mask, 1.0, 0.0), axis=1, keepdims=True) * (blocks / rows)
        tails[mask] = jnp.where(lane == COUNT_LANE, count, 0.0) if mask % 2 else jnp.broadcast_to(count, lane.shape)
    for g in range(width // group):
        cut = slice(g * group, (g + 1) * group)
        outer = jnp.dot(factors, v_ref[:, cut], preferred_element_type=F32)
        for mask in range(slots):
            high, low = mask * rank, (slots + mask) * rank
            value = outer[high : high + rank] + outer[low : low + rank]
            if mask % 2:
                code = scale_code(jnp.max(jnp.abs(value), axis=1, keepdims=True))
                send_ref[mask // 2, :, cut] = to_code(value, code)
                tails[mask] = jnp.where(lane == g, code, tails[mask])
            else:
                keep_ref[mask // 2, :, cut] = value
    for mask in range(slots):
        if mask % 2:
            send_ref[mask // 2, :, width:] = tails[mask].astype(I32).astype(I16)
        else:
            keep_ref[mask // 2, :, width:] = tails[mask]


def table_sums(place, v, ranks, blocks, slots):
    rows, width = v.shape
    rank = ranks[0].shape[0]
    half = slots // 2
    return pl.pallas_call(
        functools.partial(table_kernel, blocks, slots),
        in_specs=whole(2 + len(ranks)),
        out_specs=whole(2),
        out_shape=[
            jax.ShapeDtypeStruct((half, rank, width + LANES), I16),
            jax.ShapeDtypeStruct((half, rank, width + LANES), F32),
        ],
        compiler_params=params(16),
        cost_estimate=cost(WORK, 0),
        name="table_sums",
    )(place, v, *ranks)


def combine_kernel(tables, *refs):
    keeps, gots, (own_ref, *sends) = refs[:tables], refs[tables : 2 * tables], refs[2 * tables :]
    start = 0
    for keep_ref, got_ref in zip(keeps, gots):
        wide = keep_ref.shape[2]
        width = wide - LANES
        for j in range(keep_ref.shape[0]):
            value, count = decode_rows(got_ref, j, width)
            value = value + keep_ref[j, :, :width]
            count = count + keep_ref[j, :, width : width + 1]
            if j == 0:
                own_ref[0, :, start : start + width] = value
                own_ref[0, :, start + width : start + wide] = jnp.broadcast_to(count, (count.shape[0], LANES))
            else:
                encode_rows(value, count, sends[j - 1], 0, start)
        start += wide


def combine(keeps, gots):
    half, rank, _ = keeps[0].shape
    wide = sum(k.shape[2] for k in keeps)
    return pl.pallas_call(
        functools.partial(combine_kernel, len(keeps)),
        in_specs=whole(2 * len(keeps)),
        out_specs=whole(half),
        out_shape=[jax.ShapeDtypeStruct((1, rank, wide), F32)]
        + [jax.ShapeDtypeStruct((1, rank, wide), I16)] * (half - 1),
        compiler_params=params(16),
        cost_estimate=cost(WORK, 0),
        name="combine",
    )(*keeps, *gots)


def finish_kernel(block_length, tables, own_ref, *refs):
    gots, outs = refs[:-tables], refs[-tables:]
    start = 0
    for out_ref in outs:
        width = out_ref.shape[2]
        value = own_ref[0, :, start : start + width]
        count = own_ref[0, :, start + width : start + width + 1]
        for got in gots:
            more, further = decode_rows(got, 0, width, start)
            value, count = value + more, count + further
        out_ref[0] = value * (2.0 / jnp.maximum(count * float(block_length), 1.0))
        start += width + LANES


def finish(own, gots, block_length, widths):
    _, rank, wide = own.shape
    return pl.pallas_call(
        functools.partial(finish_kernel, block_length, len(widths)),
        in_specs=whole(1 + len(gots)),
        out_specs=whole(len(widths)),
        out_shape=[jax.ShapeDtypeStruct((1, rank, width), F32) for width in widths],
        compiler_params=params(16),
        cost_estimate=cost(WORK, 0),
        name="finish",
    )(own, *gots)


def through_kernel(cots, terms, pieces, first, place_ref, *refs):
    cot_refs, refs = refs[:cots], refs[cots:]
    w_ref, refs = refs[0], refs[1:]
    ranks, refs = refs[:terms], refs[terms:]
    maps, (out_ref, factors) = refs[:pieces], refs[-2:]
    width, block = cot_refs[0].shape[1], out_ref.shape[1]

    @pl.when(pl.program_id(0) == 0)
    def _():
        masks = gather_masks(sum(p.shape[0] for p in maps))
        factors[...] = both_parts(2.0 * rank_total(ranks), place_ref[...], masks).T.astype(BF16)

    here = pl.ds(pl.multiple_of((first + pl.program_id(0)) * block, block), block)
    rows = stacked(maps, here)
    total = jnp.dot(factors[...], jnp.concatenate([rows, rows], axis=0), preferred_element_type=F32)
    for i, cot in enumerate(cot_refs):
        columns = pl.ds(pl.multiple_of(owner(i) * width, width), width)
        total = total + lax.dot_general(cot[...], w_ref[here, columns], NT, preferred_element_type=F32)
    out_ref[...] = total


def through(place, cots, w, ranks, maps, start, stop, of, before=()):
    rows, width = cots[0].shape
    depth, features = w.shape
    count = sum(m.shape[0] * m.shape[1] for m in maps)
    block = depth // of
    operands = [place, *cots, w, *ranks, *maps]
    return pl.pallas_call(
        functools.partial(through_kernel, len(cots), len(ranks), len(maps), start),
        grid=(stop - start,),
        in_specs=whole(len(operands)) + [pl.BlockSpec(memory_space=pl.ANY) for _ in before],
        out_specs=pl.BlockSpec((rows, block), lambda i: (0, start + i)),
        scratch_shapes=[VM((rows, 2 * count), BF16)],
        out_shape=jax.ShapeDtypeStruct((rows, depth), F32),
        input_output_aliases={len(operands): 0} if before else {},
        compiler_params=params(16, 1),
        cost_estimate=cost(WORK, 0),
        name="through",
    )(*operands, *before)


def project_kernel(blocks, group, codes, terms, pieces, place_ref, own_ref, *refs):
    code_refs, refs = refs[:codes], refs[codes:]
    ranks, refs = refs[:terms], refs[terms:]
    maps, (out_ref, total_ref, sems) = refs[:pieces], refs[pieces:]
    masks = gather_masks(sum(p.shape[0] for p in maps))
    factors = both_parts(2.0 * rank_total(ranks), place_ref[...], masks).T.astype(BF16)
    every = stacked(maps)
    every = jnp.concatenate([every, every], axis=0)
    rows = own_ref.shape[0]
    length = rows // blocks
    copies = []
    for b in range(blocks):
        cut = slice(b * length, (b + 1) * length)
        total = own_ref[cut] + jnp.dot(factors[cut], every, preferred_element_type=F32)
        for code in code_refs:
            g = b * length // group
            scale = jnp.exp2(code[0, rows : rows + 16].astype(I32).astype(F32) * (1.0 / STEPS))
            total = total + code[0, cut].astype(I32).astype(F32) * scale[g : g + 1]
        total_ref[cut] = total
        here = pl.ds(b * length, length)
        copies.append(pltpu.make_async_copy(total_ref.at[here], out_ref.at[here], sems.at[b]))
        copies[-1].start()
    for copy in copies:
        copy.wait()


def project(place, own, codes, ranks, maps, blocks, group):
    rows, width = own.shape
    return pl.pallas_call(
        functools.partial(project_kernel, blocks, group, len(codes), len(ranks), len(maps)),
        in_specs=whole(2 + len(codes) + len(ranks) + len(maps)),
        out_specs=pl.BlockSpec(memory_space=pl.ANY),
        out_shape=jax.ShapeDtypeStruct((rows, width), F32),
        scratch_shapes=[VM((rows, width), F32), pltpu.SemaphoreType.DMA((blocks,))],
        compiler_params=params(16),
        cost_estimate=cost(0, 0),
        name="project",
    )(place, own, *codes, *ranks, *maps)


def swap(value, axis, size, mask):
    return lax.ppermute(value, axis, [(i, i ^ mask) for i in range(size)])


def after(value, earlier):
    return lax.optimization_barrier((value, earlier))[0]


def shards(reps, tps, tokens, weight, cot, maps_in, maps_out, tenant, slot_of):
    chips = tps // 2
    blocks = tenant.shape[0]
    rows = tokens.shape[0]
    length = rows // blocks
    slots = reps
    width = cot.shape[1]
    rep = lax.axis_index("rep")
    core = functools.partial(swap, axis="tp", size=tps, mask=1)

    def over_y(value, k):
        return swap(value, "tp", tps, 2 * k)

    def over_rep(value, mask):
        return swap(value, "rep", reps, mask)

    def spread(chip_sum):
        return [chip_sum] + [over_y(chip_sum, k) for k in peers]

    peers = range(1, chips)
    bits = [reps >> i for i in range(1, reps.bit_length())]
    out_held, in_held = maps_out, maps_in
    out_got = over_rep(out_held, bits[0])
    in_got = over_rep(in_held, bits[0])
    cot_y = [over_y(cot, k) for k in peers]
    place = plan(rep, tenant, slot_of, rows)
    out_got = after(out_got, place)
    for bit in bits[1:]:
        out_held = jnp.concatenate([out_held, out_got], axis=0)
        in_held = jnp.concatenate([in_held, in_got], axis=0)
        if bit == 1:
            out_held, in_held = after((out_held, in_held), sent_peer)
        out_held, in_held = lax.optimization_barrier((out_held, in_held))
        out_got, in_got = over_rep(out_held, bit), over_rep(in_held, bit)
        if bit == bits[1]:
            sent_peer = base_send(after(tokens, out_got), weight, [2 * k + 1 for k in peers], width)
    outs_all, ins_all = [out_held, out_got], [in_held, in_got]

    sent_own = base_send(after(tokens, out_held), weight, [1], width)
    got_peer, got_own = core(sent_peer), core(sent_own)
    back_part = rank_part(place, after(cot, (cot_y, sent_own)), outs_all)
    back_sum = back_part + core(back_part)
    back = spread(back_sum)
    codes = base_code(after(tokens, back_sum), weight, got_peer, [2 * k for k in peers], 128)
    forward_part = rank_part(place, after(tokens, codes[0]), ins_all)
    in_send, in_keep = table_sums(place, after(tokens, forward_part), back, blocks, slots)
    in_swapped = over_rep(in_send, 1)
    forward_sum = forward_part + after(core(forward_part), in_send)
    forward = spread(forward_sum)
    base_codes = [over_y(after(codes[k - 1], forward_sum), k) for k in peers]
    cots = []
    for piece in [cot] + cot_y:
        cots += [piece, core(after(piece, back_sum))]
    def through_part(earlier, start, stop, before):
        return through(
            place, [after(cots[0], earlier)] + cots[1:], weight, back, ins_all, start, stop, 4, before
        )

    first = through_part(forward_sum, 0, 1, [])
    out_send, out_keep = table_sums(place, after(cot, first), forward, blocks, slots)
    out_swapped = over_rep(out_send, 1)
    second = through_part(out_send, 1, 3, [first])
    grads_own, *grads = combine([in_keep, out_keep], [in_swapped, after(out_swapped, second)])
    grads_got = [over_rep(g, 2 * (j + 1)) for j, g in enumerate(grads)]
    token_grad = through_part(grads_own, 3, 4, [second])
    own_base = base_own(after(tokens, token_grad), weight, got_own)
    projected = project(place, own_base, base_codes, forward, outs_all, blocks, 128)
    grad_in, grad_out = finish(after(grads_own, projected), grads_got, length, [tokens.shape[1], width])
    return projected, token_grad, grad_in, grad_out


def solution(mesh):
    placed = (
        P("rep", "tp"),
        P("tp", None),
        P("rep", "tp"),
        P("rep", None, "tp"),
        P("rep", None, "tp"),
        P("rep"),
        P(),
    )
    return jax.shard_map(
        functools.partial(shards, mesh.shape["rep"], mesh.shape["tp"]),
        mesh=mesh,
        in_specs=placed,
        out_specs=(P("rep", "tp"), P("rep", "tp"), P("rep", None, "tp"), P("rep", None, "tp")),
        check_vma=False,
    )
```

```python
import functools

import jax
import jax.numpy as jnp
from jax import lax
from jax.experimental import pallas as pl
from jax.experimental.pallas import tpu as pltpu
from jax.sharding import PartitionSpec as P

F32, BF16, I32, I16 = jnp.float32, jnp.bfloat16, jnp.int32, jnp.int16
VM = pltpu.VMEM
STEPS = 128.0
CODE_TOP = 32767.0
LEAST = 1e-33
LANES = 128
COUNT_LANE = 64
WORK = 10e9
NT = (((1,), (1,)), ((), ()))
TN = (((0,), (0,)), ((), ()))


def params(mib, grid_dims=0):
    return pltpu.CompilerParams(
        vmem_limit_bytes=mib << 20,
        dimension_semantics=("arbitrary",) * grid_dims if grid_dims else None,
    )


def cost(flops, moved):
    return pl.CostEstimate(flops=int(flops), bytes_accessed=int(moved), transcendentals=0)


def whole(n):
    return [pl.BlockSpec(memory_space=VM)] * n


def scale_code(top):
    return jnp.ceil(STEPS * (jnp.log2(jnp.maximum(top, LEAST)) - 15.0)) + 1.0


def to_code(value, code):
    level = jnp.round(value * jnp.exp2(code * (-1.0 / STEPS)))
    return jnp.clip(level, -CODE_TOP, CODE_TOP).astype(I32).astype(I16)


def from_code(level, code):
    return level.astype(I32).astype(F32) * jnp.exp2(code.astype(I32).astype(F32) * (1.0 / STEPS))


def split(value):
    high = value.astype(BF16)
    return high, (value - high.astype(F32)).astype(BF16)


def plan_kernel(rep, tenant, slot_of, place):
    blocks = tenant.shape[0]
    length = place.shape[1] // blocks
    for b in range(blocks):
        mask = jnp.bitwise_xor(slot_of[tenant[b]], rep[0])
        place[:, b * length : (b + 1) * length] = jnp.full((1, length), mask, I32)


def plan(rep, tenant, slot_of, rows):
    smem = pl.BlockSpec(memory_space=pltpu.SMEM)
    return pl.pallas_call(
        plan_kernel,
        in_specs=[smem] * 3,
        out_specs=whole(1)[0],
        out_shape=jax.ShapeDtypeStruct((1, rows), I32),
        compiler_params=params(16),
        cost_estimate=cost(WORK, 0),
        name="plan",
    )(jnp.stack([rep, rep]).astype(I32), tenant, slot_of)


def owner(mask):
    return jnp.bitwise_xor(lax.axis_index("tp"), mask)


def pack_kernel(*refs):
    parts, (out_ref, sems) = refs[:-2], refs[-2:]
    copies, start = [], 0
    for i, part in enumerate(parts):
        here = pl.ds(start, part.shape[2])
        copies.append(pltpu.make_async_copy(part, out_ref.at[:, :, here], sems.at[i]))
        copies[-1].start()
        start += part.shape[2]
    for copy in copies:
        copy.wait()


def pack(*parts):
    total = sum(p.shape[2] for p in parts)
    return pl.pallas_call(
        pack_kernel,
        in_specs=[pl.BlockSpec(memory_space=pl.ANY)] * len(parts),
        out_specs=whole(1)[0],
        out_shape=jax.ShapeDtypeStruct(parts[0].shape[:2] + (total,), parts[0].dtype),
        scratch_shapes=[pltpu.SemaphoreType.DMA((len(parts),))],
        compiler_params=params(16),
        cost_estimate=cost(0, 0),
        name="pack",
    )(*parts)


def base_send_kernel(masks, x_ref, w_ref, out_ref):
    width = out_ref.shape[2]
    for i, mask in enumerate(masks):
        columns = pl.ds(pl.multiple_of(owner(mask) * width, width), width)
        out_ref[i] = jnp.dot(x_ref[...], w_ref[:, columns], preferred_element_type=F32)


def base_send(x, w, masks, width):
    rows, depth = x.shape
    return pl.pallas_call(
        functools.partial(base_send_kernel, masks),
        in_specs=whole(2),
        out_specs=whole(1)[0],
        out_shape=jax.ShapeDtypeStruct((len(masks), rows, width), F32),
        compiler_params=params(16),
        cost_estimate=cost(10e9, 0),
        name="base_send",
    )(x, w)


def base_own_kernel(x_ref, w_ref, got_ref, own_ref):
    width = own_ref.shape[1]
    columns = pl.ds(pl.multiple_of(owner(0) * width, width), width)
    own_ref[...] = got_ref[0] + jnp.dot(x_ref[...], w_ref[:, columns], preferred_element_type=F32)


def base_own(x, w, got):
    _, rows, width = got.shape
    return pl.pallas_call(
        base_own_kernel,
        in_specs=whole(3),
        out_specs=whole(1)[0],
        out_shape=jax.ShapeDtypeStruct((rows, width), F32),
        compiler_params=params(16),
        cost_estimate=cost(0, 0),
        name="base_own",
    )(x, w, got)


def base_code_kernel(group, masks, x_ref, w_ref, got_ref, *code_refs):
    rows, width = got_ref.shape[1:]
    block = min(256, width)
    for i, (mask, code_ref) in enumerate(zip(masks, code_refs)):
        for j in range(width // block):
            cut = slice(j * block, (j + 1) * block)
            columns = pl.ds(pl.multiple_of(owner(mask) * width + j * block, block), block)
            total = got_ref[i, :, cut] + jnp.dot(x_ref[...], w_ref[:, columns], preferred_element_type=F32)
            tail = jnp.zeros((16, block), F32)
            row = lax.broadcasted_iota(I32, tail.shape, 0)
            for g in range(rows // group):
                part = total[g * group : (g + 1) * group]
                code = scale_code(jnp.max(jnp.abs(part), axis=0, keepdims=True))
                code_ref[0, g * group : (g + 1) * group, cut] = to_code(part, code)
                tail = jnp.where(row == g, code, tail)
            code_ref[0, rows:, cut] = tail.astype(I32).astype(I16)


def base_code(x, w, got, masks, group):
    count, rows, width = got.shape
    return pl.pallas_call(
        functools.partial(base_code_kernel, group, masks),
        in_specs=whole(3),
        out_specs=whole(count),
        out_shape=[jax.ShapeDtypeStruct((1, rows + 16, width), I16)] * count,
        compiler_params=params(16),
        cost_estimate=cost(0, 0),
        name="base_code",
    )(x, w, got)


def gather_masks(count):
    return [*range(0, count, 2), *range(1, count, 2)]


def stacked(pieces, here=slice(None)):
    return jnp.concatenate([p[:, :, here].reshape(p.shape[0] * p.shape[1], -1) for p in pieces], axis=0)


def spread_rows(value, place, masks):
    return jnp.concatenate([jnp.where(place == m, value, 0.0) for m in masks], axis=0)


def rank_total(ranks):
    total = ranks[0][...]
    for term in ranks[1:]:
        total = total + term[...]
    return total


def both_parts(total, place, masks):
    high, low = split(total)
    parts = [spread_rows(part.astype(F32), place, masks) for part in (high, low)]
    return jnp.concatenate(parts, axis=0)


def rank_kernel(place_ref, v_ref, *refs):
    maps, out_ref = refs[:-1], refs[-1]
    rank = out_ref.shape[0]
    every = lax.dot_general(stacked(maps), v_ref[...], NT, preferred_element_type=F32)
    place = place_ref[...]
    total = jnp.zeros(out_ref.shape, F32)
    for i, mask in enumerate(gather_masks(every.shape[0] // rank)):
        total = jnp.where(place == mask, every[i * rank : (i + 1) * rank], total)
    out_ref[...] = total


def rank_part(place, v, maps, work):
    rank = maps[0].shape[1]
    return pl.pallas_call(
        rank_kernel,
        in_specs=whole(2 + len(maps)),
        out_specs=whole(1)[0],
        out_shape=jax.ShapeDtypeStruct((rank, v.shape[0]), F32),
        compiler_params=params(16),
        cost_estimate=cost(work, 0),
        name="rank_part",
    )(place, v, *maps)


def encode_rows(value, count, out_ref, at, start=0):
    rank, width = value.shape
    group = min(512, width)
    tail = jnp.zeros((rank, LANES), F32)
    lane = lax.broadcasted_iota(I32, tail.shape, 1)
    for g in range(width // group):
        part = value[:, g * group : (g + 1) * group]
        code = scale_code(jnp.max(jnp.abs(part), axis=1, keepdims=True))
        out_ref[at, :, start + g * group : start + (g + 1) * group] = to_code(part, code)
        tail = jnp.where(lane == g, code, tail)
    tail = jnp.where(lane == COUNT_LANE, count, tail)
    out_ref[at, :, start + width : start + width + LANES] = tail.astype(I32).astype(I16)


def decode_rows(ref, at, width, start=0):
    group = min(512, width)
    tail = ref[at, :, start + width : start + width + LANES].astype(I32).astype(F32)
    parts = []
    for g in range(width // group):
        level = ref[at, :, start + g * group : start + (g + 1) * group].astype(I32).astype(F32)
        parts.append(level * jnp.exp2(tail[:, g : g + 1] * (1.0 / STEPS)))
    return jnp.concatenate(parts, axis=1), tail[:, COUNT_LANE : COUNT_LANE + 1]


def table_kernel(blocks, slots, place_ref, v_ref, *refs):
    ranks, (send_ref, keep_ref) = refs[:-2], refs[-2:]
    place = place_ref[...]
    rows, width = v_ref.shape
    rank = ranks[0].shape[0]
    factors = both_parts(rank_total(ranks), place, range(slots)).astype(BF16)
    group = min(512, width)
    lane = lax.broadcasted_iota(I32, (rank, LANES), 1)
    tails = {}
    for mask in range(slots):
        count = jnp.sum(jnp.where(place == mask, 1.0, 0.0), axis=1, keepdims=True) * (blocks / rows)
        tails[mask] = jnp.where(lane == COUNT_LANE, count, 0.0) if mask % 2 else jnp.broadcast_to(count, lane.shape)
    for g in range(width // group):
        cut = slice(g * group, (g + 1) * group)
        outer = jnp.dot(factors, v_ref[:, cut], preferred_element_type=F32)
        for mask in range(slots):
            high, low = mask * rank, (slots + mask) * rank
            value = outer[high : high + rank] + outer[low : low + rank]
            if mask % 2:
                code = scale_code(jnp.max(jnp.abs(value), axis=1, keepdims=True))
                send_ref[mask // 2, :, cut] = to_code(value, code)
                tails[mask] = jnp.where(lane == g, code, tails[mask])
            else:
                keep_ref[mask // 2, :, cut] = value
    for mask in range(slots):
        if mask % 2:
            send_ref[mask // 2, :, width:] = tails[mask].astype(I32).astype(I16)
        else:
            keep_ref[mask // 2, :, width:] = tails[mask]


def table_sums(place, v, ranks, blocks, slots):
    rows, width = v.shape
    rank = ranks[0].shape[0]
    half = slots // 2
    return pl.pallas_call(
        functools.partial(table_kernel, blocks, slots),
        in_specs=whole(2 + len(ranks)),
        out_specs=whole(2),
        out_shape=[
            jax.ShapeDtypeStruct((half, rank, width + LANES), I16),
            jax.ShapeDtypeStruct((half, rank, width + LANES), F32),
        ],
        compiler_params=params(16),
        cost_estimate=cost(WORK, 0),
        name="table_sums",
    )(place, v, *ranks)


def combine_kernel(tables, *refs):
    keeps, gots, (own_ref, *sends) = refs[:tables], refs[tables : 2 * tables], refs[2 * tables :]
    start = 0
    for keep_ref, got_ref in zip(keeps, gots):
        wide = keep_ref.shape[2]
        width = wide - LANES
        for j in range(keep_ref.shape[0]):
            value, count = decode_rows(got_ref, j, width)
            value = value + keep_ref[j, :, :width]
            count = count + keep_ref[j, :, width : width + 1]
            if j == 0:
                own_ref[0, :, start : start + width] = value
                own_ref[0, :, start + width : start + wide] = jnp.broadcast_to(count, (count.shape[0], LANES))
            else:
                encode_rows(value, count, sends[j - 1], 0, start)
        start += wide


def combine(keeps, gots):
    half, rank, _ = keeps[0].shape
    wide = sum(k.shape[2] for k in keeps)
    return pl.pallas_call(
        functools.partial(combine_kernel, len(keeps)),
        in_specs=whole(2 * len(keeps)),
        out_specs=whole(half),
        out_shape=[jax.ShapeDtypeStruct((1, rank, wide), F32)]
        + [jax.ShapeDtypeStruct((1, rank, wide), I16)] * (half - 1),
        compiler_params=params(16),
        cost_estimate=cost(WORK, 0),
        name="combine",
    )(*keeps, *gots)


def finish_kernel(block_length, tables, own_ref, *refs):
    gots, outs = refs[:-tables], refs[-tables:]
    start = 0
    for out_ref in outs:
        width = out_ref.shape[2]
        value = own_ref[0, :, start : start + width]
        count = own_ref[0, :, start + width : start + width + 1]
        for got in gots:
            more, further = decode_rows(got, 0, width, start)
            value, count = value + more, count + further
        out_ref[0] = value * (2.0 / jnp.maximum(count * float(block_length), 1.0))
        start += width + LANES


def finish(own, gots, block_length, widths):
    _, rank, wide = own.shape
    return pl.pallas_call(
        functools.partial(finish_kernel, block_length, len(widths)),
        in_specs=whole(1 + len(gots)),
        out_specs=whole(len(widths)),
        out_shape=[jax.ShapeDtypeStruct((1, rank, width), F32) for width in widths],
        compiler_params=params(16),
        cost_estimate=cost(WORK, 0),
        name="finish",
    )(own, *gots)


def through_kernel(cots, terms, pieces, first, place_ref, *refs):
    cot_refs, refs = refs[:cots], refs[cots:]
    w_ref, refs = refs[0], refs[1:]
    ranks, refs = refs[:terms], refs[terms:]
    maps, (out_ref, factors) = refs[:pieces], refs[-2:]
    width, block = cot_refs[0].shape[1], out_ref.shape[1]

    @pl.when(pl.program_id(0) == 0)
    def _():
        masks = gather_masks(sum(p.shape[0] for p in maps))
        factors[...] = both_parts(2.0 * rank_total(ranks), place_ref[...], masks).T.astype(BF16)

    here = pl.ds(pl.multiple_of((first + pl.program_id(0)) * block, block), block)
    rows = stacked(maps, here)
    total = jnp.dot(factors[...], jnp.concatenate([rows, rows], axis=0), preferred_element_type=F32)
    for i, cot in enumerate(cot_refs):
        columns = pl.ds(pl.multiple_of(owner(i) * width, width), width)
        total = total + lax.dot_general(cot[...], w_ref[here, columns], NT, preferred_element_type=F32)
    out_ref[...] = total


def through(place, cots, w, ranks, maps, start, stop, of, before=()):
    rows, width = cots[0].shape
    depth, features = w.shape
    count = sum(m.shape[0] * m.shape[1] for m in maps)
    block = depth // of
    operands = [place, *cots, w, *ranks, *maps]
    return pl.pallas_call(
        functools.partial(through_kernel, len(cots), len(ranks), len(maps), start),
        grid=(stop - start,),
        in_specs=whole(len(operands)) + [pl.BlockSpec(memory_space=pl.ANY) for _ in before],
        out_specs=pl.BlockSpec((rows, block), lambda i: (0, start + i)),
        scratch_shapes=[VM((rows, 2 * count), BF16)],
        out_shape=jax.ShapeDtypeStruct((rows, depth), F32),
        input_output_aliases={len(operands): 0} if before else {},
        compiler_params=params(16, 1),
        cost_estimate=cost(WORK, 0),
        name="through",
    )(*operands, *before)


def project_kernel(blocks, group, codes, terms, pieces, place_ref, own_ref, *refs):
    code_refs, refs = refs[:codes], refs[codes:]
    ranks, refs = refs[:terms], refs[terms:]
    maps, (out_ref, total_ref, sems) = refs[:pieces], refs[pieces:]
    masks = gather_masks(sum(p.shape[0] for p in maps))
    factors = both_parts(2.0 * rank_total(ranks), place_ref[...], masks).T.astype(BF16)
    every = stacked(maps)
    every = jnp.concatenate([every, every], axis=0)
    rows = own_ref.shape[0]
    length = rows // blocks
    copies = []
    for b in range(blocks):
        cut = slice(b * length, (b + 1) * length)
        total = own_ref[cut] + jnp.dot(factors[cut], every, preferred_element_type=F32)
        for code in code_refs:
            g = b * length // group
            scale = jnp.exp2(code[0, rows : rows + 16].astype(I32).astype(F32) * (1.0 / STEPS))
            total = total + code[0, cut].astype(I32).astype(F32) * scale[g : g + 1]
        total_ref[cut] = total
        here = pl.ds(b * length, length)
        copies.append(pltpu.make_async_copy(total_ref.at[here], out_ref.at[here], sems.at[b]))
        copies[-1].start()
    for copy in copies:
        copy.wait()


def project(place, own, codes, ranks, maps, blocks, group):
    rows, width = own.shape
    return pl.pallas_call(
        functools.partial(project_kernel, blocks, group, len(codes), len(ranks), len(maps)),
        in_specs=whole(2 + len(codes) + len(ranks) + len(maps)),
        out_specs=pl.BlockSpec(memory_space=pl.ANY),
        out_shape=jax.ShapeDtypeStruct((rows, width), F32),
        scratch_shapes=[VM((rows, width), F32), pltpu.SemaphoreType.DMA((blocks,))],
        compiler_params=params(16),
        cost_estimate=cost(0, 0),
        name="project",
    )(place, own, *codes, *ranks, *maps)


def swap(value, axis, size, mask):
    return lax.ppermute(value, axis, [(i, i ^ mask) for i in range(size)])


def after(value, earlier):
    return lax.optimization_barrier((value, earlier))[0]


def shards(reps, tps, tokens, weight, cot, maps_in, maps_out, tenant, slot_of):
    chips = tps // 2
    blocks = tenant.shape[0]
    rows = tokens.shape[0]
    length = rows // blocks
    slots = reps
    width = cot.shape[1]
    rep = lax.axis_index("rep")
    core = functools.partial(swap, axis="tp", size=tps, mask=1)

    def over_y(value, k):
        return swap(value, "tp", tps, 2 * k)

    def over_rep(value, mask):
        return swap(value, "rep", reps, mask)

    def spread(chip_sum):
        return [chip_sum] + [over_y(chip_sum, k) for k in peers]

    peers = range(1, chips)
    cot_y = [over_y(cot, k) for k in peers]
    packed = pack(maps_out, maps_in)
    column = [packed] + [over_rep(packed, mask) for mask in range(2, reps, 2)]
    place = plan(rep, tenant, slot_of, rows)
    column = jnp.concatenate(after(column, place), axis=0)
    out_column, in_column = lax.optimization_barrier((column[:, :, :width], column[:, :, width:]))
    out_swapped_maps, in_swapped_maps = over_rep(out_column, 1), over_rep(in_column, 1)
    outs_all, ins_all = [out_column, out_swapped_maps], [in_column, in_swapped_maps]

    sent_peer = base_send(after(tokens, (out_column, in_column)), weight, [2 * k + 1 for k in peers], width)
    sent_own = base_send(after(tokens, sent_peer), weight, [1], width)
    got_peer, got_own = core(sent_peer), core(sent_own)
    back_part = rank_part(place, after(cot, sent_own), outs_all, 10e9)
    back_sum = back_part + core(back_part)
    back = spread(back_sum)
    codes = base_code(after(tokens, (back_sum, cot_y)), weight, got_peer, [2 * k for k in peers], 128)
    forward_part = rank_part(place, after(tokens, codes[0]), ins_all, WORK)
    in_send, in_keep = table_sums(place, after(tokens, forward_part), back, blocks, slots)
    in_swapped = over_rep(in_send, 1)
    forward_sum = forward_part + after(core(forward_part), in_send)
    forward = spread(forward_sum)
    base_codes = [over_y(after(codes[k - 1], forward_sum), k) for k in peers]
    cots = []
    for piece in [cot] + cot_y:
        cots += [piece, core(after(piece, back_sum))]
    def through_part(earlier, start, stop, before):
        return through(
            place, [after(cots[0], earlier)] + cots[1:], weight, back, ins_all, start, stop, 4, before
        )

    first = through_part(forward_sum, 0, 1, [])
    out_send, out_keep = table_sums(place, after(cot, first), forward, blocks, slots)
    out_swapped = over_rep(out_send, 1)
    second = through_part(out_send, 1, 3, [first])
    grads_own, *grads = combine([in_keep, out_keep], [in_swapped, after(out_swapped, second)])
    grads_got = [over_rep(g, 2 * (j + 1)) for j, g in enumerate(grads)]
    token_grad = through_part(grads_own, 3, 4, [second])
    own_base = base_own(after(tokens, token_grad), weight, got_own)
    projected = project(place, own_base, base_codes, forward, outs_all, blocks, 128)
    grad_in, grad_out = finish(after(grads_own, projected), grads_got, length, [tokens.shape[1], width])
    return projected, token_grad, grad_in, grad_out


def solution(mesh):
    placed = (
        P("rep", "tp"),
        P("tp", None),
        P("rep", "tp"),
        P("rep", None, "tp"),
        P("rep", None, "tp"),
        P("rep"),
        P(),
    )
    return jax.shard_map(
        functools.partial(shards, mesh.shape["rep"], mesh.shape["tp"]),
        mesh=mesh,
        in_specs=placed,
        out_specs=(P("rep", "tp"), P("rep", "tp"), P("rep", None, "tp"), P("rep", None, "tp")),
        check_vma=False,
    )
```
